256 devices in a mesh: dp: 16 (over x, z_hi, core), seq: 16 (over y, z_lo).
Axes of the slice: x: 4, y: 4, z: 8 (z_hi: 2, z_lo: 4; z = z_hi * 4 + z_lo), core: 2. Of those that a mesh axis runs over, the one named last changes fastest.
Arguments:
- tokens: bfloat16 [16, 2048, 1536], P('dp', 'seq'), may hold values from -6 to 6
- w_proj: bfloat16 [1536, 2304], replicated, may hold values from -1 to 1
- d_attended: bfloat16 [16, 2048, 768], P('dp', 'seq'), may hold values from -6 to 6
Outputs:
- attended: bfloat16 [16, 2048, 768], P('dp', 'seq')
- d_tokens: bfloat16 [16, 2048, 1536], P('dp', 'seq')
- grad_proj: float32 [1536, 2304], P('seq', 'dp')
The draws below stay inside these ranges and needn't reach their ends.
All inputs are finite; a program needn't handle non-finite values.
Results may differ from the reference program's by a relative error of at most 0.03.
Values may be sent and summed in bfloat16 or wider, within the bound.
No kernel may reach another device: no remote copies, remote signals or barrier semaphores. Data moves between devices by JAX's collectives and lax.ppermute only.
A program may use at most 128 MiB of HBM per device.

```python
import math
import jax
import jax.numpy as jnp
from jax import lax

D = 1536
HS = 192
HEADS = 4
TOK_DEV = 128
HD = 768
LEN = 2048
SEQS = 16


def draw_w_proj(key, part):
    key = jax.random.fold_in(key, 7)
    draw_key = jax.random.fold_in(key, 0)
    drawn = jax.random.truncated_normal(draw_key, -4.0, 4.0, (D, 3 * HD), jnp.float32)
    return jnp.clip(drawn * D ** (-0.5), -1.0, 1.0).astype(jnp.bfloat16)


def with_spikes(entries, own_key, source, target, parts, factor):
    owner, partner = [(jnp.arange(entries.shape[position]) // (entries.shape[position] // parts)).reshape([-1 if axis == position else 1 for axis in range(entries.ndim)]) for position in (source, target)]
    chosen = jax.random.permutation(own_key, parts)[partner]
    strong = (owner == chosen) | (owner == (partner + parts // 2) % parts)
    return jnp.where(strong, factor * entries, entries)


def block_scale(rng, shape, shards, least, largest):
    factor_of = 1.0
    for axis_at, parts in shards:
        heights = jax.random.uniform(jax.random.fold_in(jax.random.fold_in(rng, 6), axis_at), (parts,), jnp.float32, least / len(shards), largest / len(shards))
        factor_of = factor_of * jnp.repeat(jnp.exp(heights), shape[axis_at] // parts).reshape((-1,) + (1,) * (len(shape) - 1 - axis_at))
    return factor_of


def bell_draw_with(rng, shape, scale, reach, cuts, heavy, held_as=jnp.bfloat16):
    entries = scale * jax.random.normal(rng, shape, jnp.float32)
    if cuts:
        entries = entries * block_scale(rng, shape, cuts, -0.22, 0.18)
    return jnp.clip(with_spikes(entries, jax.random.fold_in(rng, 3), *heavy), -reach, reach).astype(held_as)


def setup_inputs(seed: int = 0) -> dict:
    key_list = jax.random.split(jax.random.key(seed), 4)
    return {
        "tokens": bell_draw_with(key_list[0], (SEQS, LEN, D), 1.0, 6.0, ((0, 16), (1, 16)), (1, 2, 16, 2.0)),
        "w_proj": draw_w_proj(jax.random.fold_in(key_list[3], 71), 0),
        "d_attended": bell_draw_with(key_list[2], (SEQS, LEN, HD), 1.0, 6.0, ((0, 16), (1, 16)), (0, 2, 16, 2.0)),
    }


EPS = 1e-06

def split_heads(rows):
    return rows.reshape(rows.shape[0], HEADS, -1).transpose(1, 0, 2)

def join_heads(stacked):
    return stacked.transpose(1, 0, 2).reshape(stacked.shape[1], -1)

def one_sequence(w_proj, tok_rows, grad_rows):
    score_scale = 1.0 / math.sqrt(HS)
    inputs = tok_rows.astype(jnp.float32)
    inverse = lax.rsqrt(lax.optimization_barrier(jnp.mean(inputs * inputs, -1, keepdims=True)) + EPS)
    normed = (inputs * inverse).astype(jnp.bfloat16)
    projected = jnp.dot(normed, w_proj, preferred_element_type=jnp.float32).astype(jnp.bfloat16)
    queries = split_heads(projected[:, :HD]).astype(jnp.float32)
    keys_all = split_heads(projected[:, HD:2 * HD]).astype(jnp.float32)
    values = split_heads(projected[:, 2 * HD:]).astype(jnp.float32)
    scores = jnp.einsum('hqd,hkd->hqk', queries, keys_all) * score_scale
    softmaxed = jax.nn.softmax(scores, axis=-1)
    weights = softmaxed.astype(jnp.bfloat16).astype(jnp.float32)
    attended = join_heads(jnp.einsum('hqk,hkd->hqd', weights, values)).astype(jnp.bfloat16)
    grads_out = split_heads(grad_rows).astype(jnp.float32)
    d_probs = jnp.einsum('hqd,hkd->hqk', grads_out, values)
    row_total = lax.optimization_barrier(jnp.sum(softmaxed * d_probs, -1, keepdims=True))
    d_scores = (softmaxed * (d_probs - row_total) * score_scale).astype(jnp.bfloat16).astype(jnp.float32)
    d_queries = jnp.einsum('hqk,hkd->hqd', d_scores, keys_all)
    blocks = tok_rows.shape[0] // TOK_DEV
    score_blocks = d_scores.reshape(HEADS, blocks, TOK_DEV, -1)
    query_blocks = queries.reshape(HEADS, blocks, TOK_DEV, -1)
    weight_blocks = weights.reshape(HEADS, blocks, TOK_DEV, -1)
    out_blocks = grads_out.reshape(HEADS, blocks, TOK_DEV, -1)
    key_parts = jnp.einsum('hbqk,hbqd->bhkd', score_blocks, query_blocks)
    value_parts = jnp.einsum('hbqk,hbqd->bhkd', weight_blocks, out_blocks)
    key_parts = lax.optimization_barrier(key_parts.astype(jnp.bfloat16)).astype(jnp.float32)
    value_parts = lax.optimization_barrier(value_parts.astype(jnp.bfloat16)).astype(jnp.float32)
    d_keys = lax.optimization_barrier(jnp.sum(key_parts, 0))
    d_values = lax.optimization_barrier(jnp.sum(value_parts, 0))
    d_proj = jnp.concatenate([join_heads(d_queries), join_heads(d_keys), join_heads(d_values)], 1).astype(jnp.bfloat16)
    d_normed = jnp.dot(d_proj, w_proj.T, preferred_element_type=jnp.float32)
    unrounded = inputs * inverse
    d_tokens = (inverse * (d_normed - unrounded * lax.optimization_barrier(jnp.mean(d_normed * unrounded, -1, keepdims=True)))).astype(jnp.bfloat16)
    grad_term = jnp.dot(normed.T, d_proj, preferred_element_type=jnp.float32)
    return (attended, d_tokens, grad_term)

def reference(tokens, w_proj, d_attended):

    def scan_step(grad_total, inputs_pair):
        attended, d_tokens, grad_term = one_sequence(w_proj, inputs_pair[0], inputs_pair[1])
        return (grad_total + grad_term, (attended, d_tokens))
    zero_grads = jnp.zeros((w_proj.shape[0], w_proj.shape[1]), jnp.float32)
    grad_total, outputs = lax.scan(scan_step, zero_grads, (tokens, d_attended))
    return (outputs[0], outputs[1], grad_total)
```

```python
import math

import jax
import jax.numpy as jnp
from jax import lax
from jax.experimental import pallas as pl
from jax.experimental.pallas import tpu as pltpu
from jax.sharding import Mesh
from jax.sharding import PartitionSpec as P

HS = 192
HEADS = 4
HD = 768
D = 1536
ROWS = 128
EPS = 1e-06
SCALE = 1.0 / math.sqrt(HS)
SCALE2 = SCALE * math.log2(math.e)
BF = jnp.bfloat16
F32 = jnp.float32
NN = (((1,), (0,)), ((), ()))
NT = (((1,), (1,)), ((), ()))

SMEM = pl.BlockSpec(memory_space=pltpu.SMEM)


def shape(dims, dtype=BF):
    return jax.ShapeDtypeStruct(dims, dtype)


def params():
    return pltpu.CompilerParams(vmem_limit_bytes=48 * 2**20)


def dot(a, b, dims=NN):
    return lax.dot_general(a, b, dims, preferred_element_type=F32)


def flip(block):
    return jnp.transpose(block.astype(F32))


def normalise(tokens):
    rows = tokens.astype(F32)
    inverse = lax.rsqrt(jnp.mean(rows * rows, -1, keepdims=True) + EPS)
    return rows * inverse, inverse


def project_kernel(place, tokens, weights, grads, normed, *rest):
    kv, qd, cut = rest[:4], rest[4:8], rest[8]
    step = pl.program_id(0)

    @pl.when(step == 0)
    def _():
        normed[...] = normalise(tokens[...])[0].astype(BF)
        turned = flip(grads[...]).astype(BF)
        for head in range(HEADS):
            cut[head, 3 * HS :, :] = turned[head * HS : (head + 1) * HS]

    turned = flip(dot(normed[...], weights[...])).astype(BF)
    at = pl.ds(pl.multiple_of(step * HS, HS), HS)
    for head in range(HEADS):
        cut[head, at, :] = turned[head * HS : (head + 1) * HS]

    @pl.when(step == 2)
    def _():
        for k in range(4):
            head = lax.rem(place[0] + k, 4)
            kv[k][...] = cut[head, : 2 * HS, :]
            qd[k][...] = cut[head, 2 * HS :, :]


def project(place, tokens, weights, grads):
    whole = lambda dims: pl.BlockSpec(dims, lambda i: (0, 0))
    half = (2 * HS, ROWS)
    return pl.pallas_call(
        project_kernel,
        grid=(3,),
        in_specs=[
            SMEM,
            whole((ROWS, D)),
            pl.BlockSpec((D, HD), lambda i: (0, lax.rem(i + 1, 3))),
            whole((ROWS, HD)),
        ],
        out_specs=[whole((ROWS, D))] + [whole(half)] * 8,
        out_shape=[shape((ROWS, D))] + [shape(half)] * 8,
        scratch_shapes=[pltpu.VMEM((HEADS, 4 * HS, ROWS), BF)],
        compiler_params=params(),
        name="project",
    )(place, tokens, weights, grads)


def side_by_side(blocks, wide):
    for k, block in enumerate(blocks):
        wide[:, k * ROWS : (k + 1) * ROWS] = block[...]


TILE = 256


def stats_kernel(*refs):
    kv_blocks, qd_blocks, stats, kv, qd = refs[:8], refs[8:16], refs[16], refs[17], refs[18]
    side_by_side(kv_blocks, kv)
    side_by_side(qd_blocks, qd)
    keys = flip(kv[:HS, :]).astype(BF)
    values = flip(kv[HS:, :]).astype(BF)
    for tile in range(8 * ROWS // TILE):
        at = slice(tile * TILE, (tile + 1) * TILE)
        scores = dot(keys, qd[:HS, at]) * SCALE2
        top = jnp.max(scores, 0, keepdims=True)
        powers = jnp.exp2(scores - top)
        d_probs = dot(values, qd[HS:, at])
        stats[0:1, at] = top
        stats[1:2, at] = jnp.sum(powers, 0, keepdims=True)
        stats[2:3, at] = jnp.sum(powers * d_probs, 0, keepdims=True)
        stats[3:8, at] = jnp.zeros((5, TILE), F32)


def stats_of(kv_blocks, qd_blocks):
    wide = pltpu.VMEM((2 * HS, 8 * ROWS), BF)
    return pl.pallas_call(
        stats_kernel,
        out_shape=shape((8, 8 * ROWS), F32),
        scratch_shapes=[wide, wide],
        compiler_params=params(),
        name="stats",
    )(*kv_blocks, *qd_blocks)


def attend_kernel(*refs):
    kv_blocks, qd_blocks, mine, theirs = refs[:8], refs[8:16], refs[16], refs[17]
    qo_own, qo_send, kv_own, kv_send, kv, qd, kv_sum = refs[18:]
    side_by_side(kv_blocks, kv)
    side_by_side(qd_blocks, qd)
    keys = flip(kv[:HS, :]).astype(BF)
    values = flip(kv[HS:, :]).astype(BF)
    half = 4 * ROWS
    for tile in range(8 * ROWS // TILE):
        at = slice(tile * TILE, (tile + 1) * TILE)
        start = (tile * TILE + half) % (2 * half)
        across = slice(start, start + TILE)
        top_a, sum_a, total_a = mine[0:1, at], mine[1:2, at], mine[2:3, at]
        top_b, sum_b, total_b = theirs[0:1, across], theirs[1:2, across], theirs[2:3, across]
        top = jnp.maximum(top_a, top_b)
        by_a, by_b = jnp.exp2(top_a - top), jnp.exp2(top_b - top)
        share = 1.0 / (sum_a * by_a + sum_b * by_b)
        row_total = (total_a * by_a + total_b * by_b) * share
        scores = dot(keys, qd[:HS, at]) * SCALE2
        softmaxed = jnp.exp2(scores - top) * share
        d_probs = dot(values, qd[HS:, at])
        d_scores = (softmaxed * (d_probs - row_total) * SCALE).astype(BF)
        weights = softmaxed.astype(BF)
        d_queries = dot(kv[:HS, :], d_scores)
        attended = dot(kv[HS:, :], weights)
        if tile * TILE < half:
            qo_own[:HS, at] = d_queries
            qo_own[HS:, at] = attended
        else:
            qo_send[:HS, across] = d_queries.astype(BF)
            qo_send[HS:, across] = attended.astype(BF)
        d_keys = dot(qd[:HS, at], d_scores, NT)
        d_values = dot(qd[HS:, at], weights, NT)
        if tile == 0:
            kv_sum[:HS, :] = d_keys
            kv_sum[HS:, :] = d_values
        else:
            kv_sum[:HS, :] += d_keys
            kv_sum[HS:, :] += d_values
    kv_own[...] = kv_sum[:, :half]
    kv_send[...] = kv_sum[:, half:].astype(BF)


def attend(kv_blocks, qd_blocks, mine, theirs):
    wide = (2 * HS, 8 * ROWS)
    out = (2 * HS, 4 * ROWS)
    return pl.pallas_call(
        attend_kernel,
        out_shape=[shape(out, F32), shape(out), shape(out, F32), shape(out)],
        scratch_shapes=[pltpu.VMEM(wide, BF), pltpu.VMEM(wide, BF), pltpu.VMEM(wide, F32)],
        compiler_params=params(),
        name="attend",
    )(*kv_blocks, *qd_blocks, mine, theirs)


def gradient_kernel(place, qo_own, qo_got, kv_own, kv_got, *refs):
    normed_blocks, back, keep, send, normed, d_proj, cut = (
        refs[:4], refs[4:8], refs[8], refs[9], refs[10], refs[11], refs[12],
    )
    for k, block in enumerate(normed_blocks):
        normed[k * ROWS : (k + 1) * ROWS, :] = block[...]
    q_sum = qo_own[...] + qo_got[...].astype(F32)
    kv_sum = kv_own[...] + kv_got[...].astype(F32)
    d_proj[:HS, :] = q_sum[:HS].astype(BF)
    d_proj[HS : 3 * HS, :] = kv_sum.astype(BF)
    attended = q_sum[HS:].astype(BF)
    for k in range(4):
        at = slice(k * ROWS, (k + 1) * ROWS)
        back[k][: 3 * HS, :] = d_proj[:, at]
        back[k][3 * HS :, :] = attended[:, at]
    for j in range(3):
        term = dot(d_proj[j * HS : (j + 1) * HS, :], normed[...]).astype(BF)
        for i in range(4):
            cut[i % 2, 2 * j + i // 2] = term[i * 48 : (i + 1) * 48]
    keep[...] = cut[place[2]]
    send[...] = cut[1 - place[2]]


def gradient(place, qo_own, qo_got, kv_own, kv_got, normed_blocks):
    units = (6, 48, D)
    vmem = pl.BlockSpec(memory_space=pltpu.VMEM)
    return pl.pallas_call(
        gradient_kernel,
        in_specs=[SMEM] + [vmem] * 8,
        out_shape=[shape((4 * HS, ROWS))] * 4 + [shape(units)] * 2,
        scratch_shapes=[
            pltpu.VMEM((4 * ROWS, D), BF),
            pltpu.VMEM((3 * HS, 4 * ROWS), BF),
            pltpu.VMEM((2,) + units, BF),
        ],
        compiler_params=params(),
        name="gradient",
    )(place, qo_own, qo_got, kv_own, kv_got, *normed_blocks)


def tokens_kernel(place, tokens, weights, *refs):
    blocks, attended, d_tokens, columns, d_proj, d_normed = (
        refs[:4], refs[4], refs[5], refs[6], refs[7], refs[8],
    )
    step = pl.program_id(0)

    @pl.when(step == 0)
    def _():
        for k in range(4):
            head = lax.rem(place[0] + k, 4)
            for j in range(4):
                at = pl.ds(pl.multiple_of(j * HD + head * HS, HS), HS)
                columns[at, :] = blocks[k][j * HS : (j + 1) * HS, :]
        d_proj[...] = flip(columns[: 3 * HD, :]).astype(BF)
        attended[...] = flip(columns[3 * HD :, :]).astype(BF)

    d_normed[step] = dot(d_proj[...], weights[...], NT)

    @pl.when(step == pl.num_programs(0) - 1)
    def _():
        unrounded, inverse = normalise(tokens[...])
        parts = range(d_normed.shape[0])
        wide = d_normed.shape[2]
        total = sum(
            jnp.sum(d_normed[i] * unrounded[:, i * wide : (i + 1) * wide], -1, keepdims=True)
            for i in parts
        )
        mean = total * (1.0 / D)
        for i in parts:
            at = slice(i * wide, (i + 1) * wide)
            d_tokens[:, at] = (inverse * (d_normed[i] - unrounded[:, at] * mean)).astype(BF)


def tokens_of(place, tokens, weights, blocks):
    whole = lambda dims: pl.BlockSpec(dims, lambda i: (0, 0))
    tile = 256
    return pl.pallas_call(
        tokens_kernel,
        grid=(D // tile,),
        in_specs=[SMEM, whole((ROWS, D)), pl.BlockSpec((tile, 3 * HD), lambda i: (i, 0))]
        + [whole((4 * HS, ROWS))] * 4,
        out_specs=[whole((ROWS, HD)), whole((ROWS, D))],
        out_shape=[shape((ROWS, HD)), shape((ROWS, D))],
        scratch_shapes=[
            pltpu.VMEM((4 * HD, ROWS), BF),
            pltpu.VMEM((ROWS, 3 * HD), BF),
            pltpu.VMEM((D // tile, ROWS, tile), F32),
        ],
        compiler_params=params(),
        name="d_tokens",
    )(place, tokens, weights, *blocks)


def small(kernel, name, place, blocks, outs, scratch):
    vmem = pl.BlockSpec(memory_space=pltpu.VMEM)
    return pl.pallas_call(
        kernel,
        in_specs=[SMEM] + [vmem] * len(blocks),
        out_shape=outs,
        scratch_shapes=scratch,
        compiler_params=params(),
        name=name,
    )(place, *blocks)


def split_y_kernel(place, mine, got, *refs):
    outs, cut = refs[:4], refs[4]
    cut[...] = (mine[...].astype(F32) + got[...].astype(F32)).astype(BF)
    for k in range(4):
        at = pl.ds(pl.multiple_of(lax.rem(place[1] + k, 4) * 384, 384), 384)
        outs[k][...] = cut[:, :, at]


def split_z_kernel(place, *refs):
    blocks, outs, cut = refs[:4], refs[4:8], refs[8]
    total = sum(block[...].astype(F32) for block in blocks)
    for k in range(4):
        cut[k] = total[:, :, k * 96 : (k + 1) * 96].astype(BF)
    for k in range(4):
        outs[k][...] = cut[lax.rem(place[0] + k, 4)]


def split_x_kernel(place, *refs):
    blocks, outs, cut = refs[:4], refs[4:8], refs[8]
    for k in range(4):
        head = lax.rem(place[0] + 4 - k, 4)
        for j in range(3):
            cut[pl.ds((j * 4 + head) * 2, 2)] = blocks[k][2 * j : 2 * j + 2]
    for k in range(4):
        outs[k][...] = cut[pl.ds(lax.rem(place[3] + k, 4) * 6, 6)]


def split_zh_kernel(place, *refs):
    blocks, keep, send, cut = refs[:4], refs[4], refs[5], refs[6]
    cut[...] = sum(block[...].astype(F32) for block in blocks)
    keep[...] = cut[pl.ds(place[4] * 3, 3)]
    send[...] = cut[pl.ds(3 - place[4] * 3, 3)].astype(BF)


def split_c_kernel(place, mine, got, keep, send):
    keep[...] = mine[...] + got[...].astype(F32)
    send[...] = keep[2 - 2 * place[2]].astype(BF)


def finish_kernel(place, mine, got, out):
    core = place[2]
    rows = jnp.concatenate([mine[core], got[...].astype(F32), mine[1 + core]], 0)
    out[...] = jnp.transpose(rows)


def shift(size, by):
    return [(i, (i + by) % size) for i in range(size)]


def per_device(tokens, w_proj, d_attended):
    tokens = tokens[0]
    place = jnp.stack([lax.axis_index(a) for a in ("zl", "y", "c", "x", "zh")]).astype(jnp.int32)
    near = [(0, 1), (1, 0), (2, 3), (3, 2)]
    far = [(0, 3), (3, 0), (1, 2), (2, 1)]
    swap = [(0, 1), (1, 0)]

    def spread(blocks, axis, way=1):
        return [blocks[0]] + [lax.ppermute(blocks[k], axis, shift(4, way * k)) for k in (1, 2, 3)]

    normed, *cuts = project(place, tokens, w_proj, d_attended[0])
    kv = spread(cuts[:4], "zl")
    qd = spread(cuts[4:], "zl")
    kv_far = [lax.ppermute(b, "y", far) for b in kv]
    qd_near = [lax.ppermute(b, "y", near) for b in qd]
    held = lax.optimization_barrier((normed, *kv, *qd))[0]
    normed_all = [normed] + [lax.ppermute(held, "zl", shift(4, k)) for k in (1, 2, 3)]

    kv, qd = kv + kv_far, qd + qd_near
    mine = stats_of(kv, qd)
    theirs = lax.ppermute(mine, "y", near)
    qo_own, qo_send, kv_own, kv_send = attend(kv, qd, mine, theirs)
    qo_got = lax.ppermute(qo_send, "y", near)
    kv_got = lax.ppermute(kv_send, "y", far)

    *back, keep, send = gradient(place, qo_own, qo_got, kv_own, kv_got, normed_all)
    got = lax.ppermute(send, "c", swap)
    blocks = small(
        split_y_kernel, "split_y", place, [keep, got],
        [shape((6, 48, 384))] * 4, [pltpu.VMEM((6, 48, D), BF)],
    )
    blocks = spread(blocks, "y")
    blocks = small(
        split_z_kernel, "split_z", place, blocks,
        [shape((6, 48, 96))] * 4, [pltpu.VMEM((4, 6, 48, 96), BF)],
    )
    blocks = spread(blocks, "zl")
    blocks = small(
        split_x_kernel, "split_x", place, blocks,
        [shape((6, 48, 96))] * 4, [pltpu.VMEM((24, 48, 96), BF)],
    )
    blocks = spread(blocks, "x")
    keep, send = small(
        split_zh_kernel, "split_zh", place, blocks,
        [shape((3, 48, 96), F32), shape((3, 48, 96))], [pltpu.VMEM((6, 48, 96), F32)],
    )
    got = lax.ppermute(send, "zh", swap)
    keep, send = small(
        split_c_kernel, "split_c", place, [keep, got],
        [shape((3, 48, 96), F32), shape((48, 96))], [],
    )
    got = lax.ppermute(send, "c", swap)
    grad = small(finish_kernel, "finish", place, [keep, got], shape((96, 144), F32), [])

    returned = spread(back, "zl", -1)
    attended, d_tokens = tokens_of(place, tokens, w_proj, returned)
    return (attended[None], d_tokens[None], grad)


def solution(mesh):
    fine = Mesh(mesh.devices.reshape(4, 2, 2, 4, 4), ("x", "zh", "c", "y", "zl"))
    dp, seq = ("x", "zh", "c"), ("y", "zl")
    return jax.shard_map(
        per_device,
        mesh=fine,
        in_specs=(P(dp, seq, None), P(), P(dp, seq, None)),
        out_specs=(P(dp, seq, None), P(dp, seq, None), P(seq, dp)),
        check_vma=False,
    )
```

```python
import math

import jax
import jax.numpy as jnp
from jax import lax
from jax.experimental import pallas as pl
from jax.experimental.pallas import tpu as pltpu
from jax.sharding import Mesh
from jax.sharding import PartitionSpec as P

HS = 192
HEADS = 4
HD = 768
D = 1536
ROWS = 128
EPS = 1e-06
SCALE = 1.0 / math.sqrt(HS)
SCALE2 = SCALE * math.log2(math.e)
BF = jnp.bfloat16
F32 = jnp.float32
NN = (((1,), (0,)), ((), ()))
NT = (((1,), (1,)), ((), ()))

SMEM = pl.BlockSpec(memory_space=pltpu.SMEM)
VMEM = pl.BlockSpec(memory_space=pltpu.VMEM)
ANY = pl.BlockSpec(memory_space=pl.ANY)
HBM = pl.BlockSpec(memory_space=pltpu.HBM)


def shape(dims, dtype=BF):
    return jax.ShapeDtypeStruct(dims, dtype)


def params(mib=16):
    return pltpu.CompilerParams(vmem_limit_bytes=mib * 2**20)


def dot(a, b, dims=NN):
    return lax.dot_general(a, b, dims, preferred_element_type=F32)


def flip(block):
    return jnp.transpose(block.astype(F32))


def normalise(tokens):
    rows = tokens.astype(F32)
    inverse = lax.rsqrt(jnp.mean(rows * rows, -1, keepdims=True) + EPS)
    return rows * inverse, inverse


CUT = 256
CUTS = 3 * HD // CUT


def project_kernel(place, tokens_in, weights_in, grads_in, *rest):
    blocks, (tokens, weights, grads, turned, sems) = rest[:4], rest[4:]
    fetches = [pltpu.make_async_copy(tokens_in, tokens, sems.at[0])]
    for n in range(CUTS):
        at = slice(n * CUT, (n + 1) * CUT)
        fetches.append(pltpu.make_async_copy(weights_in.at[:, at], weights.at[n], sems.at[n + 1]))
    fetches.append(pltpu.make_async_copy(grads_in, grads, sems.at[CUTS + 1]))
    for fetch in fetches:
        fetch.start()
    fetches[0].wait()
    rows = normalise(tokens[...])[0].astype(BF)
    last = None
    for n in range(CUTS):
        fetches[n + 1].wait()
        part = dot(rows, weights[n])
        if last is not None:
            turned[(n - 1) * CUT : n * CUT, :] = flip(last).astype(BF)
        last = part
    turned[3 * HD - CUT : 3 * HD, :] = flip(last).astype(BF)
    fetches[-1].wait()
    turned[3 * HD :, :] = flip(grads[...]).astype(BF)
    for k in range(4):
        head = place[0] ^ k
        for n, j in enumerate((1, 2, 0, 3)):
            at = pl.ds(pl.multiple_of(j * HD + head * HS, 64), HS)
            blocks[k][n * HS : (n + 1) * HS, :] = turned[at, :]


def project(place, tokens, weights, grads):
    return pl.pallas_call(
        project_kernel,
        in_specs=[SMEM, HBM, HBM, HBM],
        out_shape=[shape((4 * HS, ROWS))] * 4,
        scratch_shapes=[
            pltpu.VMEM((ROWS, D), BF),
            pltpu.VMEM((CUTS, D, CUT), BF),
            pltpu.VMEM((ROWS, HD), BF),
            pltpu.VMEM((4 * HD, ROWS), BF),
            pltpu.SemaphoreType.DMA((CUTS + 2,)),
        ],
        compiler_params=params(60),
        name="project",
    )(place, tokens, weights, grads)


def stack_kernel(*refs):
    kv, qd = refs[-2:]
    for k, block in enumerate(refs[:4]):
        at = slice(k * ROWS, (k + 1) * ROWS)
        kv[:, at] = block[: 2 * HS, :]
        qd[:, at] = block[2 * HS :, :]


def stack(blocks, after):
    return pl.pallas_call(
        stack_kernel,
        in_specs=[VMEM] * 4 + [ANY] * len(after),
        out_shape=[shape((2 * HS, 4 * ROWS))] * 2,
        compiler_params=params(),
        name="stack",
    )(*blocks, *after)


def side_by_side(blocks, wide):
    for k, block in enumerate(blocks):
        wide[:, k * 4 * ROWS : (k + 1) * 4 * ROWS] = block[...]


TILE = 256


def stats_kernel(*refs):
    kv_blocks, qd_blocks, (stats, kv, qd) = refs[:2], refs[2:4], refs[-3:]
    side_by_side(kv_blocks, kv)
    side_by_side(qd_blocks, qd)
    keys = flip(kv[:HS, :]).astype(BF)
    values = flip(kv[HS:, :]).astype(BF)
    for tile in range(8 * ROWS // TILE):
        at = slice(tile * TILE, (tile + 1) * TILE)
        scores = dot(keys, qd[:HS, at]) * SCALE2
        top = jnp.max(scores, 0, keepdims=True)
        powers = jnp.exp2(scores - top)
        d_probs = dot(values, qd[HS:, at])
        stats[0:1, at] = top
        stats[1:2, at] = jnp.sum(powers, 0, keepdims=True)
        stats[2:3, at] = jnp.sum(powers * d_probs, 0, keepdims=True)
        stats[3:8, at] = jnp.zeros((5, TILE), F32)


def stats_of(kv_blocks, qd_blocks):
    wide = pltpu.VMEM((2 * HS, 8 * ROWS), BF)
    return pl.pallas_call(
        stats_kernel,
        out_shape=shape((8, 8 * ROWS), F32),
        scratch_shapes=[wide, wide],
        compiler_params=params(),
        name="stats",
    )(*kv_blocks, *qd_blocks)


def attend_kernel(*refs):
    kv_blocks, qd_blocks, mine, theirs = refs[:2], refs[2:4], refs[4], refs[5]
    qo_own, qo_send, kv_own, kv_send, kv, qd, kv_sum = refs[-7:]
    side_by_side(kv_blocks, kv)
    side_by_side(qd_blocks, qd)
    keys = flip(kv[:HS, :]).astype(BF)
    values = flip(kv[HS:, :]).astype(BF)
    half = 4 * ROWS
    for tile in range(8 * ROWS // TILE):
        at = slice(tile * TILE, (tile + 1) * TILE)
        start = (tile * TILE + half) % (2 * half)
        across = slice(start, start + TILE)
        top_a, sum_a, total_a = mine[0:1, at], mine[1:2, at], mine[2:3, at]
        top_b, sum_b, total_b = theirs[0:1, across], theirs[1:2, across], theirs[2:3, across]
        top = jnp.maximum(top_a, top_b)
        by_a, by_b = jnp.exp2(top_a - top), jnp.exp2(top_b - top)
        share = 1.0 / (sum_a * by_a + sum_b * by_b)
        row_total = (total_a * by_a + total_b * by_b) * share
        scores = dot(keys, qd[:HS, at]) * SCALE2
        softmaxed = jnp.exp2(scores - top) * share
        d_probs = dot(values, qd[HS:, at])
        d_scores = (softmaxed * (d_probs - row_total) * SCALE).astype(BF)
        weights = softmaxed.astype(BF)
        d_queries = dot(kv[:HS, :], d_scores)
        attended = dot(kv[HS:, :], weights)
        if tile * TILE < half:
            qo_own[:HS, at] = d_queries
            qo_own[HS:, at] = attended
        else:
            qo_send[:HS, across] = d_queries.astype(BF)
            qo_send[HS:, across] = attended.astype(BF)
        d_keys = dot(qd[:HS, at], d_scores, NT)
        d_values = dot(qd[HS:, at], weights, NT)
        if tile == 0:
            kv_sum[:HS, :] = d_keys
            kv_sum[HS:, :] = d_values
        else:
            kv_sum[:HS, :] += d_keys
            kv_sum[HS:, :] += d_values
    kv_own[...] = kv_sum[:, :half]
    kv_send[...] = kv_sum[:, half:].astype(BF)


def attend(kv_blocks, qd_blocks, mine, theirs, after):
    wide = (2 * HS, 8 * ROWS)
    out = (2 * HS, 4 * ROWS)
    return pl.pallas_call(
        attend_kernel,
        in_specs=[VMEM] * (6 + len(after)),
        out_shape=[shape(out, F32), shape(out), shape(out, F32), shape(out)],
        scratch_shapes=[pltpu.VMEM(wide, BF), pltpu.VMEM(wide, BF), pltpu.VMEM(wide, F32)],
        compiler_params=params(24),
        name="attend",
    )(*kv_blocks, *qd_blocks, mine, theirs, *after)


def gradient_kernel(place, qo_own, qo_got, kv_own, kv_got, *refs):
    own, pair, second, middle, ends = refs[:5]
    back, (keep, send, normed, d_proj, cut) = refs[5:9], refs[9:]
    at_end = (place[0] == 0) | (place[0] == 3)
    third = jnp.where(at_end, ends[...], middle[...])
    for k, block in enumerate((own[...], pair[...], second[...], third)):
        normed[k * ROWS : (k + 1) * ROWS, :] = normalise(block)[0].astype(BF)
    q_sum = qo_own[...] + qo_got[...].astype(F32)
    kv_sum = kv_own[...] + kv_got[...].astype(F32)
    d_proj[:HS, :] = q_sum[:HS].astype(BF)
    d_proj[HS : 3 * HS, :] = kv_sum.astype(BF)
    attended = q_sum[HS:].astype(BF)
    for k in range(4):
        at = slice(k * ROWS, (k + 1) * ROWS)
        back[k][: 3 * HS, :] = d_proj[:, at]
        back[k][3 * HS :, :] = attended[:, at]
    counts = [jnp.int32(0), jnp.int32(0)]
    for j in range(3):
        at = slice(j * HS, (j + 1) * HS)
        term = dot(d_proj[at, :], normed[...]).astype(BF)
        for i in range(4):
            unit = 16 * j + 4 * place[0] + i
            core = lax.rem(lax.div(unit, 3), 2)
            slot = jnp.where(core == 0, counts[0], counts[1])
            cut[core, slot] = term[i * 48 : (i + 1) * 48]
            counts = [counts[0] + (1 - core), counts[1] + core]
    keep[...] = cut[place[2]]
    send[...] = cut[1 - place[2]]


def gradient(place, qo_own, qo_got, kv_own, kv_got, tokens):
    units = (6, 48, D)
    return pl.pallas_call(
        gradient_kernel,
        in_specs=[SMEM] + [VMEM] * 9,
        out_shape=[shape((4 * HS, ROWS))] * 4 + [shape(units)] * 2,
        scratch_shapes=[
            pltpu.VMEM((4 * ROWS, D), BF),
            pltpu.VMEM((3 * HS, 4 * ROWS), BF),
            pltpu.VMEM((2,) + units, BF),
        ],
        compiler_params=params(),
        name="gradient",
    )(place, qo_own, qo_got, kv_own, kv_got, *tokens)


WIDE = 512


def tokens_kernel(place, tokens, weights, *refs):
    blocks, (attended, d_tokens, done, columns, d_normed) = refs[:4], refs[4:]
    done[...] = jnp.zeros_like(done)
    for k in range(4):
        head = place[0] ^ k
        for j in range(4):
            at = pl.ds(pl.multiple_of(j * HD + head * HS, 64), HS)
            columns[at, :] = blocks[k][j * HS : (j + 1) * HS, :]
    attended[...] = flip(columns[3 * HD :, :]).astype(BF)
    d_proj = columns[: 3 * HD, :]
    unrounded, inverse = normalise(tokens[...])
    total = jnp.zeros((ROWS, 1), F32)
    for n in range(D // WIDE):
        at = slice(n * WIDE, (n + 1) * WIDE)
        part = jnp.transpose(dot(weights[at, :], d_proj))
        d_normed[:, at] = part
        total += jnp.sum(part * unrounded[:, at], -1, keepdims=True)
    d_tokens[...] = (inverse * (d_normed[...] - unrounded * (total * (1.0 / D)))).astype(BF)


def tokens_of(place, tokens, weights, blocks):
    return pl.pallas_call(
        tokens_kernel,
        in_specs=[SMEM] + [VMEM] * 6,
        out_shape=[shape((ROWS, HD)), shape((ROWS, D)), shape((8, 128), F32)],
        scratch_shapes=[
            pltpu.VMEM((4 * HD, ROWS), BF),
            pltpu.VMEM((ROWS, D), F32),
        ],
        compiler_params=params(20),
        name="d_tokens",
    )(place, tokens, weights, *blocks)


def small(kernel, name, scalars, blocks, outs, scratch, after=()):
    return pl.pallas_call(
        kernel,
        in_specs=[SMEM] * len(scalars) + [VMEM] * (len(blocks) + len(after)),
        out_shape=outs,
        scratch_shapes=scratch,
        compiler_params=params(),
        name=name,
    )(*scalars, *blocks, *after)


def split_y_kernel(place, mine, got, *refs):
    outs, cut = refs[:4], refs[4]
    cut[...] = (mine[...].astype(F32) + got[...].astype(F32)).astype(BF)
    for k in range(4):
        at = pl.ds(pl.multiple_of((place[1] ^ k) * 384, 384), 384)
        outs[k][...] = cut[:, :, at]


def split_z_kernel(place, *refs):
    blocks, outs, cut = refs[:4], refs[4:8], refs[8]
    total = sum(block[...].astype(F32) for block in blocks)
    for k in range(4):
        cut[k] = total[:, :, k * 96 : (k + 1) * 96].astype(BF)
    for k in range(4):
        outs[k][...] = cut[place[0] ^ k]


def lists():
    tables = []
    for core in range(2):
        count, table = [0] * HEADS, []
        for slot in range(24):
            head = (6 * (slot // 3) + 3 * core + slot % 3) % 16 // 4
            table.append((head, count[head]))
            count[head] += 1
        tables.append(table)
    return list(zip(*tables))


def split_x_kernel(place, *refs):
    blocks, outs, by_head, cut = refs[:4], refs[4:8], refs[8], refs[9]
    for k in range(4):
        by_head[place[0] ^ k] = blocks[k][...]
    for slot, (first, second) in enumerate(lists()):
        head, at = (jnp.where(place[2] == 0, a, b) for a, b in zip(first, second))
        cut[slot] = by_head[head, at]
    for k in range(4):
        outs[k][...] = cut[pl.ds((place[3] ^ k) * 6, 6)]


def split_zh_kernel(place, *refs):
    blocks, (keep, send, cut) = refs[:4], refs[-3:]
    cut[...] = sum(block[...].astype(F32) for block in blocks)
    keep[...] = cut[pl.ds(place[4] * 3, 3)]
    send[...] = cut[pl.ds(3 - place[4] * 3, 3)].astype(BF)


def finish_kernel(place, mine, got, out):
    out[...] = (mine[...] + got[...].astype(F32)).reshape(144, 96)


def exchange(by):
    return [(i, i ^ by) for i in range(4)]


def per_device(tokens, w_proj, d_attended):
    tokens = tokens[0]
    place = jnp.stack([lax.axis_index(a) for a in ("zl", "y", "c", "x", "zh")]).astype(jnp.int32)
    near, far, swap = exchange(1), exchange(3), [(0, 1), (1, 0)]

    def spread(blocks, axis):
        return [blocks[0]] + [lax.ppermute(blocks[k], axis, exchange(k)) for k in (1, 2, 3)]

    pair = lax.ppermute(tokens, "zl", near)
    middle = lax.ppermute(tokens, "zl", [(1, 2), (2, 1)])
    heads = spread(project(place, tokens, w_proj, d_attended[0]), "zl")
    kv, qd = stack(heads, [pair, middle])
    late = lax.optimization_barrier((tokens, kv))[0]
    second = lax.ppermute(late, "zl", exchange(2))
    ends = lax.ppermute(late, "zl", [(0, 3), (3, 0)])
    kv, qd = [kv, lax.ppermute(kv, "y", far)], [qd, lax.ppermute(qd, "y", near)]

    mine = stats_of(kv, qd)
    theirs = lax.ppermute(mine, "y", near)
    qo_own, qo_send, kv_own, kv_send = attend(kv, qd, mine, theirs, [ends])
    qo_got = lax.ppermute(qo_send, "y", near)
    kv_got = lax.ppermute(kv_send, "y", far)

    rows = [tokens, pair, second, middle, ends]
    *back, keep, send = gradient(place, qo_own, qo_got, kv_own, kv_got, rows)
    returned = [back[0], lax.ppermute(back[1], "zl", near)]
    later = lax.optimization_barrier((back[2], back[3], returned[1]))
    returned += [lax.ppermute(later[k - 2], "zl", exchange(k)) for k in (2, 3)]
    attended, d_tokens, done = tokens_of(place, tokens, w_proj, returned)
    got = lax.ppermute(send, "c", swap)
    blocks = small(
        split_y_kernel, "split_y", [place], [keep, got],
        [shape((6, 48, 384))] * 4, [pltpu.VMEM((6, 48, D), BF)],
    )
    blocks = spread(blocks, "y")
    blocks = small(
        split_z_kernel, "split_z", [place], blocks,
        [shape((6, 48, 96))] * 4, [pltpu.VMEM((4, 6, 48, 96), BF)],
    )
    blocks = spread(blocks, "zl")
    blocks = small(
        split_x_kernel, "split_x", [place], blocks,
        [shape((6, 48, 96))] * 4,
        [pltpu.VMEM((4, 6, 48, 96), BF), pltpu.VMEM((24, 48, 96), BF)],
    )
    blocks = spread(blocks, "x")
    keep, send = small(
        split_zh_kernel, "split_zh", [place], blocks,
        [shape((3, 48, 96), F32), shape((3, 48, 96))], [pltpu.VMEM((6, 48, 96), F32)], [done],
    )
    got = lax.ppermute(send, "zh", swap)
    grad = small(finish_kernel, "finish", [place], [keep, got], shape((144, 96), F32), [])
    return (attended[None], d_tokens[None], grad.T)


def solution(mesh):
    fine = Mesh(mesh.devices.reshape(4, 2, 2, 4, 4), ("x", "zh", "c", "y", "zl"))
    dp, seq = ("x", "zh", "c"), ("y", "zl")
    return jax.shard_map(
        per_device,
        mesh=fine,
        in_specs=(P(dp, seq, None), P(), P(dp, seq, None)),
        out_specs=(P(dp, seq, None), P(dp, seq, None), P(seq, dp)),
        check_vma=False,
    )
```

```python
import math

import jax
import jax.numpy as jnp
from jax import lax
from jax.experimental import pallas as pl
from jax.experimental.pallas import tpu as pltpu
from jax.sharding import Mesh
from jax.sharding import PartitionSpec as P

HS = 192
HEADS = 4
HD = 768
D = 1536
ROWS = 128
EPS = 1e-06
SCALE = 1.0 / math.sqrt(HS)
SCALE2 = SCALE * math.log2(math.e)
BF = jnp.bfloat16
F32 = jnp.float32
NN = (((1,), (0,)), ((), ()))
NT = (((1,), (1,)), ((), ()))

VMEM = pl.BlockSpec(memory_space=pltpu.VMEM)
ANY = pl.BlockSpec(memory_space=pl.ANY)
HBM = pl.BlockSpec(memory_space=pltpu.HBM)


def shape(dims, dtype=BF):
    return jax.ShapeDtypeStruct(dims, dtype)


class Place:
    def __getitem__(self, n):
        return lax.axis_index(("zl", "y", "c", "x", "zh")[n])


place = Place()


def params(mib=16):
    return pltpu.CompilerParams(vmem_limit_bytes=mib * 2**20)


def dot(a, b, dims=NN):
    return lax.dot_general(a, b, dims, preferred_element_type=F32)


def flip(block):
    return jnp.transpose(block.astype(F32))


def normalise(tokens):
    rows = tokens.astype(F32)
    inverse = lax.rsqrt(jnp.mean(rows * rows, -1, keepdims=True) + EPS)
    return rows * inverse, inverse


def project_kernel(tokens_in, weights_in, grads_in, *rest):
    blocks, (tokens, weights, grads, turned, sems) = rest[:4], rest[4:]
    fetches = [pltpu.make_async_copy(tokens_in, tokens, sems.at[0])]
    for j in range(3):
        at = slice(j * HD, (j + 1) * HD)
        fetches.append(pltpu.make_async_copy(weights_in.at[:, at], weights.at[j], sems.at[j + 1]))
    fetches.append(pltpu.make_async_copy(grads_in, grads, sems.at[4]))
    for fetch in fetches:
        fetch.start()
    fetches[0].wait()
    rows = normalise(tokens[...])[0].astype(BF)
    for j in range(3):
        fetches[j + 1].wait()
        turned[j * HD : (j + 1) * HD, :] = flip(dot(rows, weights[j])).astype(BF)
    fetches[4].wait()
    turned[3 * HD :, :] = flip(grads[...]).astype(BF)
    for k in range(4):
        head = place[0] ^ k
        for n, j in enumerate((1, 2, 0, 3)):
            at = pl.ds(pl.multiple_of(j * HD + head * HS, 64), HS)
            blocks[k][n * HS : (n + 1) * HS, :] = turned[at, :]


def project(tokens, weights, grads):
    return pl.pallas_call(
        project_kernel,
        in_specs=[HBM, HBM, HBM],
        out_shape=[shape((4 * HS, ROWS))] * 4,
        scratch_shapes=[
            pltpu.VMEM((ROWS, D), BF),
            pltpu.VMEM((3, D, HD), BF),
            pltpu.VMEM((ROWS, HD), BF),
            pltpu.VMEM((4 * HD, ROWS), BF),
            pltpu.SemaphoreType.DMA((5,)),
        ],
        compiler_params=pltpu.CompilerParams(vmem_limit_bytes=62_520_000),
        name="project",
    )(tokens, weights, grads)


def stack_kernel(*refs):
    kv, qd = refs[-2:]
    for k, block in enumerate(refs[:4]):
        at = slice(k * ROWS, (k + 1) * ROWS)
        kv[:, at] = block[: 2 * HS, :]
        qd[:, at] = block[2 * HS :, :]


def stack(blocks, after):
    return pl.pallas_call(
        stack_kernel,
        in_specs=[VMEM] * 4 + [ANY] * len(after),
        out_shape=[shape((2 * HS, 4 * ROWS))] * 2,
        compiler_params=params(),
        name="stack",
    )(*blocks, *after)


def side_by_side(blocks, wide):
    for k, block in enumerate(blocks):
        wide[:, k * 4 * ROWS : (k + 1) * 4 * ROWS] = block[...]


TILE = 256


def stats_kernel(*refs):
    kv_blocks, qd_blocks, (stats, kv, qd) = refs[:2], refs[2:4], refs[-3:]
    side_by_side(kv_blocks, kv)
    side_by_side(qd_blocks, qd)
    keys = flip(kv[:HS, :]).astype(BF)
    values = flip(kv[HS:, :]).astype(BF)
    for tile in range(8 * ROWS // TILE):
        at = slice(tile * TILE, (tile + 1) * TILE)
        scores = dot(keys, qd[:HS, at]) * SCALE2
        top = jnp.max(scores, 0, keepdims=True)
        powers = jnp.exp2(scores - top)
        d_probs = dot(values, qd[HS:, at])
        stats[0:1, at] = top
        stats[1:2, at] = jnp.sum(powers, 0, keepdims=True)
        stats[2:3, at] = jnp.sum(powers * d_probs, 0, keepdims=True)
        stats[3:8, at] = jnp.zeros((5, TILE), F32)


def stats_of(kv_blocks, qd_blocks):
    wide = pltpu.VMEM((2 * HS, 8 * ROWS), BF)
    return pl.pallas_call(
        stats_kernel,
        out_shape=shape((8, 8 * ROWS), F32),
        scratch_shapes=[wide, wide],
        compiler_params=params(),
        name="stats",
    )(*kv_blocks, *qd_blocks)


def attend_kernel(*refs):
    kv_blocks, qd_blocks, mine, theirs = refs[:2], refs[2:4], refs[4], refs[5]
    qo_own, qo_send, kv_own, kv_send, kv, qd, kv_sum = refs[-7:]
    side_by_side(kv_blocks, kv)
    side_by_side(qd_blocks, qd)
    keys = flip(kv[:HS, :]).astype(BF)
    values = flip(kv[HS:, :]).astype(BF)
    half = 4 * ROWS
    for tile in range(8 * ROWS // TILE):
        at = slice(tile * TILE, (tile + 1) * TILE)
        start = (tile * TILE + half) % (2 * half)
        across = slice(start, start + TILE)
        top_a, sum_a, total_a = mine[0:1, at], mine[1:2, at], mine[2:3, at]
        top_b, sum_b, total_b = theirs[0:1, across], theirs[1:2, across], theirs[2:3, across]
        top = jnp.maximum(top_a, top_b)
        by_a, by_b = jnp.exp2(top_a - top), jnp.exp2(top_b - top)
        share = 1.0 / (sum_a * by_a + sum_b * by_b)
        row_total = (total_a * by_a + total_b * by_b) * share
        scores = dot(keys, qd[:HS, at]) * SCALE2
        softmaxed = jnp.exp2(scores - top) * share
        d_probs = dot(values, qd[HS:, at])
        d_scores = (softmaxed * (d_probs - row_total) * SCALE).astype(BF)
        weights = softmaxed.astype(BF)
        d_queries = dot(kv[:HS, :], d_scores)
        attended = dot(kv[HS:, :], weights)
        if tile * TILE < half:
            qo_own[:HS, at] = d_queries
            qo_own[HS:, at] = attended
        else:
            qo_send[:HS, across] = d_queries.astype(BF)
            qo_send[HS:, across] = attended.astype(BF)
        d_keys = dot(qd[:HS, at], d_scores, NT)
        d_values = dot(qd[HS:, at], weights, NT)
        if tile == 0:
            kv_sum[:HS, :] = d_keys
            kv_sum[HS:, :] = d_values
        else:
            kv_sum[:HS, :] += d_keys
            kv_sum[HS:, :] += d_values
    kv_own[...] = kv_sum[:, :half]
    kv_send[...] = kv_sum[:, half:].astype(BF)


def attend(kv_blocks, qd_blocks, mine, theirs, after):
    wide = (2 * HS, 8 * ROWS)
    out = (2 * HS, 4 * ROWS)
    return pl.pallas_call(
        attend_kernel,
        in_specs=[VMEM] * (6 + len(after)),
        out_shape=[shape(out, F32), shape(out), shape(out, F32), shape(out)],
        scratch_shapes=[pltpu.VMEM(wide, BF), pltpu.VMEM(wide, BF), pltpu.VMEM(wide, F32)],
        compiler_params=params(24),
        name="attend",
    )(*kv_blocks, *qd_blocks, mine, theirs, *after)


def gradient_kernel(qo_own, qo_got, kv_own, kv_got, *refs):
    own, pair, second, middle, ends = refs[:5]
    back, (keep, send, normed, d_proj, cut) = refs[5:9], refs[9:]
    at_end = (place[0] == 0) | (place[0] == 3)
    third = jnp.where(at_end, ends[...], middle[...])
    for k, block in enumerate((own[...], pair[...], second[...], third)):
        normed[k * ROWS : (k + 1) * ROWS, :] = normalise(block)[0].astype(BF)
    q_sum = qo_own[...] + qo_got[...].astype(F32)
    kv_sum = kv_own[...] + kv_got[...].astype(F32)
    d_proj[:HS, :] = q_sum[:HS].astype(BF)
    d_proj[HS : 3 * HS, :] = kv_sum.astype(BF)
    attended = q_sum[HS:].astype(BF)
    for k in range(4):
        at = slice(k * ROWS, (k + 1) * ROWS)
        back[k][: 3 * HS, :] = d_proj[:, at]
        back[k][3 * HS :, :] = attended[:, at]
    counts = [jnp.int32(0), jnp.int32(0)]
    for j in range(3):
        at = slice(j * HS, (j + 1) * HS)
        term = dot(d_proj[at, :], normed[...]).astype(BF)
        for i in range(4):
            unit = 16 * j + 4 * place[0] + i
            core = lax.rem(lax.div(unit, 3), 2)
            slot = jnp.where(core == 0, counts[0], counts[1])
            cut[core, slot] = term[i * 48 : (i + 1) * 48]
            counts = [counts[0] + (1 - core), counts[1] + core]
    keep[...] = cut[place[2]]
    send[...] = cut[1 - place[2]]


def gradient(qo_own, qo_got, kv_own, kv_got, tokens):
    units = (6, 48, D)
    return pl.pallas_call(
        gradient_kernel,
        in_specs=[VMEM] * 9,
        out_shape=[shape((4 * HS, ROWS))] * 4 + [shape(units)] * 2,
        scratch_shapes=[
            pltpu.VMEM((4 * ROWS, D), BF),
            pltpu.VMEM((3 * HS, 4 * ROWS), BF),
            pltpu.VMEM((2,) + units, BF),
        ],
        compiler_params=params(),
        name="gradient",
    )(qo_own, qo_got, kv_own, kv_got, *tokens)


WIDE = 512


def tokens_kernel(tokens, weights, *refs):
    blocks, (attended, d_tokens, done, columns, d_normed) = refs[:4], refs[4:]
    done[...] = jnp.zeros_like(done)
    for k in range(4):
        head = place[0] ^ k
        for j in range(4):
            at = pl.ds(pl.multiple_of(j * HD + head * HS, 64), HS)
            columns[at, :] = blocks[k][j * HS : (j + 1) * HS, :]
    attended[...] = flip(columns[3 * HD :, :]).astype(BF)
    d_proj = columns[: 3 * HD, :]
    unrounded, inverse = normalise(tokens[...])
    total = jnp.zeros((ROWS, 1), F32)
    for n in range(D // WIDE):
        at = slice(n * WIDE, (n + 1) * WIDE)
        part = jnp.transpose(dot(weights[at, :], d_proj))
        d_normed[:, at] = part
        total += jnp.sum(part * unrounded[:, at], -1, keepdims=True)
    d_tokens[...] = (inverse * (d_normed[...] - unrounded * (total * (1.0 / D)))).astype(BF)


def tokens_of(tokens, weights, blocks):
    return pl.pallas_call(
        tokens_kernel,
        in_specs=[VMEM] * 6,
        out_shape=[shape((ROWS, HD)), shape((ROWS, D)), shape((8, 128), F32)],
        scratch_shapes=[
            pltpu.VMEM((4 * HD, ROWS), BF),
            pltpu.VMEM((ROWS, D), F32),
        ],
        compiler_params=params(20),
        name="d_tokens",
    )(tokens, weights, *blocks)


def small(kernel, name, blocks, outs, scratch, after=()):
    return pl.pallas_call(
        kernel,
        in_specs=[VMEM] * (len(blocks) + len(after)),
        out_shape=outs,
        scratch_shapes=scratch,
        compiler_params=params(),
        name=name,
    )(*blocks, *after)


def split_y_kernel(mine, got, *refs):
    outs, cut = refs[:4], refs[4]
    cut[...] = (mine[...].astype(F32) + got[...].astype(F32)).astype(BF)
    for k in range(4):
        at = pl.ds(pl.multiple_of((place[1] ^ k) * 384, 384), 384)
        outs[k][...] = cut[:, :, at]


def ends_high(place):
    bits = jnp.int32(0)
    for head in range(HEADS):
        for core in range(2):
            units = [u for u in range(48) if u % 16 // 4 == head and u // 3 % 2 == core]
            value = sum((u // 6 % 2) << n for n, u in enumerate(units))
            bits = jnp.where((place[0] == head) & (place[2] == core), value, bits)
    return bits


def split_z_kernel(*refs):
    blocks, outs, cut = refs[:4], refs[4:8], refs[8]
    total = sum(block[...].astype(F32) for block in blocks)
    for k in range(4):
        cut[k] = total[:, :, k * 96 : (k + 1) * 96].astype(BF)
    bits = ends_high(place)
    for n in range(6):
        mirror = 3 * (((bits >> n) & 1) ^ place[4])
        for k in range(4):
            outs[k][n] = cut[place[0] ^ k ^ mirror, n]


def lists():
    tables = []
    for core in range(2):
        count, table = [0] * HEADS, []
        for slot in range(24):
            head = (6 * (slot // 3) + 3 * core + slot % 3) % 16 // 4
            table.append((head, count[head]))
            count[head] += 1
        tables.append(table)
    return list(zip(*tables))


def split_x_kernel(*refs):
    blocks, outs, by_head, cut = refs[:4], refs[4:8], refs[8], refs[9]
    for k in range(4):
        by_head[place[0] ^ k] = blocks[k][...]
    for slot, (first, second) in enumerate(lists()):
        head, at = (jnp.where(place[2] == 0, a, b) for a, b in zip(first, second))
        cut[slot] = by_head[head, at]
    for k in range(4):
        outs[k][...] = cut[pl.ds((place[3] ^ k) * 6, 6)]


def split_zh_kernel(*refs):
    blocks, (keep, send, cut) = refs[:4], refs[-3:]
    cut[...] = sum(block[...].astype(F32) for block in blocks)
    keep[...] = cut[pl.ds(place[4] * 3, 3)]
    send[...] = cut[pl.ds(3 - place[4] * 3, 3)].astype(BF)


def finish_kernel(mine, got, out):
    out[...] = (mine[...] + got[...].astype(F32)).reshape(144, 96)


def exchange(by):
    return [(i, i ^ by) for i in range(4)]


def per_device(tokens, w_proj, d_attended):
    tokens = tokens[0]
    near, far, swap = exchange(1), exchange(3), [(0, 1), (1, 0)]

    def spread(blocks, axis):
        return [blocks[0]] + [lax.ppermute(blocks[k], axis, exchange(k)) for k in (1, 2, 3)]

    pair = lax.ppermute(tokens, "zl", near)
    middle = lax.ppermute(tokens, "zl", [(1, 2), (2, 1)])
    heads = spread(project(tokens, w_proj, d_attended[0]), "zl")
    kv, qd = stack(heads, [pair, middle])
    late = lax.optimization_barrier((tokens, kv))[0]
    second = lax.ppermute(late, "zl", exchange(2))
    ends = lax.ppermute(late, "zl", [(0, 3), (3, 0)])
    kv, qd = [kv, lax.ppermute(kv, "y", far)], [qd, lax.ppermute(qd, "y", near)]

    mine = stats_of(kv, qd)
    theirs = lax.ppermute(mine, "y", near)
    qo_own, qo_send, kv_own, kv_send = attend(kv, qd, mine, theirs, [ends])
    qo_got = lax.ppermute(qo_send, "y", near)
    kv_got = lax.ppermute(kv_send, "y", far)

    rows = [tokens, pair, second, middle, ends]
    *back, keep, send = gradient(qo_own, qo_got, kv_own, kv_got, rows)
    last = lax.ppermute(back[3], "zl", exchange(3))
    later = lax.optimization_barrier((back[1], back[2], last))
    returned = [back[0]] + [lax.ppermute(later[k - 1], "zl", exchange(k)) for k in (1, 2)] + [last]
    attended, d_tokens, done = tokens_of(tokens, w_proj, returned)
    got = lax.ppermute(send, "c", swap)
    blocks = small(
        split_y_kernel, "split_y", [keep, got],
        [shape((6, 48, 384))] * 4, [pltpu.VMEM((6, 48, D), BF)],
    )
    blocks = spread(blocks, "y")
    blocks = small(
        split_z_kernel, "split_z", blocks,
        [shape((6, 48, 96))] * 4, [pltpu.VMEM((4, 6, 48, 96), BF)],
    )
    blocks = spread(blocks, "zl")
    blocks = small(
        split_x_kernel, "split_x", blocks,
        [shape((6, 48, 96))] * 4,
        [pltpu.VMEM((4, 6, 48, 96), BF), pltpu.VMEM((24, 48, 96), BF)],
    )
    blocks = spread(blocks, "x")
    keep, send = small(
        split_zh_kernel, "split_zh", blocks,
        [shape((3, 48, 96), F32), shape((3, 48, 96))], [pltpu.VMEM((6, 48, 96), F32)], [done],
    )
    got = lax.ppermute(send, ("zh", "zl"), [(z, 7 - z) for z in range(8)])
    grad = small(finish_kernel, "finish", [keep, got], shape((144, 96), F32), [])
    return (attended[None], d_tokens[None], grad.T)


def solution(mesh):
    fine = Mesh(mesh.devices.reshape(4, 2, 2, 4, 4), ("x", "zh", "c", "y", "zl"))
    dp, seq = ("x", "zh", "c"), ("y", "zl")
    return jax.shard_map(
        per_device,
        mesh=fine,
        in_specs=(P(dp, seq, None), P(), P(dp, seq, None)),
        out_specs=(P(dp, seq, None), P(dp, seq, None), P(seq, dp)),
        check_vma=False,
    )
```

```python
import math

import jax
import jax.numpy as jnp
from jax import lax
from jax.experimental import pallas as pl
from jax.experimental.pallas import tpu as pltpu
from jax.sharding import Mesh
from jax.sharding import PartitionSpec as P

HS = 192
HEADS = 4
HD = 768
D = 1536
ROWS = 128
EPS = 1e-06
SCALE = 1.0 / math.sqrt(HS)
SCALE2 = SCALE * math.log2(math.e)
BF = jnp.bfloat16
F32 = jnp.float32
NN = (((1,), (0,)), ((), ()))
NT = (((1,), (1,)), ((), ()))

VMEM = pl.BlockSpec(memory_space=pltpu.VMEM)
ANY = pl.BlockSpec(memory_space=pl.ANY)
HBM = pl.BlockSpec(memory_space=pltpu.HBM)


def shape(dims, dtype=BF):
    return jax.ShapeDtypeStruct(dims, dtype)


class Place:
    def __getitem__(self, n):
        return lax.axis_index(("zl", "y", "c", "x", "zh")[n])


place = Place()


def params(mib=16):
    return pltpu.CompilerParams(vmem_limit_bytes=mib * 2**20)


def dot(a, b, dims=NN):
    return lax.dot_general(a, b, dims, preferred_element_type=F32)


def flip(block):
    return jnp.transpose(block.astype(F32))


def normalise(tokens):
    rows = tokens.astype(F32)
    inverse = lax.rsqrt(jnp.mean(rows * rows, -1, keepdims=True) + EPS)
    return rows * inverse, inverse


def project_kernel(tokens_in, weights_in, grads_in, *rest):
    blocks, (tokens, weights, grads, turned, sems) = rest[:4], rest[4:]
    fetches = [pltpu.make_async_copy(tokens_in, tokens, sems.at[0])]
    for j in range(3):
        at = slice(j * HD, (j + 1) * HD)
        fetches.append(pltpu.make_async_copy(weights_in.at[:, at], weights.at[j], sems.at[j + 1]))
    fetches.append(pltpu.make_async_copy(grads_in, grads, sems.at[4]))
    for fetch in fetches:
        fetch.start()
    fetches[0].wait()
    rows = normalise(tokens[...])[0].astype(BF)
    for j in range(3):
        fetches[j + 1].wait()
        turned[j * HD : (j + 1) * HD, :] = flip(dot(rows, weights[j])).astype(BF)
    fetches[4].wait()
    turned[3 * HD :, :] = flip(grads[...]).astype(BF)
    for k in range(4):
        head = place[0] ^ k
        for n, j in enumerate((1, 2, 0, 3)):
            at = pl.ds(pl.multiple_of(j * HD + head * HS, 64), HS)
            blocks[k][n * HS : (n + 1) * HS, :] = turned[at, :]


def project(tokens, weights, grads):
    return pl.pallas_call(
        project_kernel,
        in_specs=[HBM, HBM, HBM],
        out_specs=[VMEM] * 4,
        out_shape=[shape((4 * HS, ROWS))] * 4,
        scratch_shapes=[
            pltpu.VMEM((ROWS, D), BF),
            pltpu.VMEM((3, D, HD), BF),
            pltpu.VMEM((ROWS, HD), BF),
            pltpu.VMEM((4 * HD, ROWS), BF),
            pltpu.SemaphoreType.DMA((5,)),
        ],
        compiler_params=pltpu.CompilerParams(vmem_limit_bytes=62_520_000),
        name="project",
    )(tokens, weights, grads)


def stack_kernel(*refs):
    kv, qd = refs[-2:]
    for k, block in enumerate(refs[:2]):
        at = slice(k * ROWS, (k + 1) * ROWS)
        kv[:, at] = block[: 2 * HS, :]
        qd[:, at] = block[2 * HS :, :]


def stack(blocks, after=()):
    return pl.pallas_call(
        stack_kernel,
        in_specs=[VMEM] * 2 + [ANY] * len(after),
        out_shape=[shape((2 * HS, 2 * ROWS))] * 2,
        compiler_params=params(),
        name="stack",
    )(*blocks, *after)


def side_by_side(blocks, wide):
    for k, block in enumerate(blocks):
        wide[:, k * 2 * ROWS : (k + 1) * 2 * ROWS] = block[...]


TILE = 256


def stats_kernel(*refs):
    kv_blocks, qd_blocks, (stats, kv, qd) = refs[:4], refs[4:8], refs[-3:]
    side_by_side(kv_blocks, kv)
    side_by_side(qd_blocks, qd)
    keys = flip(kv[:HS, :]).astype(BF)
    values = flip(kv[HS:, :]).astype(BF)
    for tile in range(8 * ROWS // TILE):
        at = slice(tile * TILE, (tile + 1) * TILE)
        scores = dot(keys, qd[:HS, at]) * SCALE2
        top = jnp.max(scores, 0, keepdims=True)
        powers = jnp.exp2(scores - top)
        d_probs = dot(values, qd[HS:, at])
        stats[0:1, at] = top
        stats[1:2, at] = jnp.sum(powers, 0, keepdims=True)
        stats[2:3, at] = jnp.sum(powers * d_probs, 0, keepdims=True)
        stats[3:8, at] = jnp.zeros((5, TILE), F32)


def stats_of(kv_blocks, qd_blocks):
    wide = pltpu.VMEM((2 * HS, 8 * ROWS), BF)
    return pl.pallas_call(
        stats_kernel,
        out_shape=shape((8, 8 * ROWS), F32),
        scratch_shapes=[wide, wide],
        compiler_params=params(),
        name="stats",
    )(*kv_blocks, *qd_blocks)


def attend_kernel(*refs):
    kv_blocks, qd_blocks, mine, theirs = refs[:4], refs[4:8], refs[8], refs[9]
    qo_own, qo_send, kv_own, kv_send, kv, qd, kv_sum = refs[-7:]
    side_by_side(kv_blocks, kv)
    side_by_side(qd_blocks, qd)
    keys = flip(kv[:HS, :]).astype(BF)
    values = flip(kv[HS:, :]).astype(BF)
    half = 4 * ROWS
    for tile in range(8 * ROWS // TILE):
        at = slice(tile * TILE, (tile + 1) * TILE)
        start = (tile * TILE + half) % (2 * half)
        across = slice(start, start + TILE)
        top_a, sum_a, total_a = mine[0:1, at], mine[1:2, at], mine[2:3, at]
        top_b, sum_b, total_b = theirs[0:1, across], theirs[1:2, across], theirs[2:3, across]
        top = jnp.maximum(top_a, top_b)
        by_a, by_b = jnp.exp2(top_a - top), jnp.exp2(top_b - top)
        share = 1.0 / (sum_a * by_a + sum_b * by_b)
        row_total = (total_a * by_a + total_b * by_b) * share
        scores = dot(keys, qd[:HS, at]) * SCALE2
        softmaxed = jnp.exp2(scores - top) * share
        d_probs = dot(values, qd[HS:, at])
        d_scores = (softmaxed * (d_probs - row_total) * SCALE).astype(BF)
        weights = softmaxed.astype(BF)
        d_queries = dot(kv[:HS, :], d_scores)
        attended = dot(kv[HS:, :], weights)
        if tile * TILE < half:
            qo_own[:HS, at] = d_queries
            qo_own[HS:, at] = attended
        else:
            qo_send[:HS, across] = d_queries.astype(BF)
            qo_send[HS:, across] = attended.astype(BF)
        d_keys = dot(qd[:HS, at], d_scores, NT)
        d_values = dot(qd[HS:, at], weights, NT)
        if tile == 0:
            kv_sum[:HS, :] = d_keys
            kv_sum[HS:, :] = d_values
        else:
            kv_sum[:HS, :] += d_keys
            kv_sum[HS:, :] += d_values
    kv_own[...] = kv_sum[:, :half]
    kv_send[...] = kv_sum[:, half:].astype(BF)


def attend(kv_blocks, qd_blocks, mine, theirs, after):
    wide = (2 * HS, 8 * ROWS)
    out = (2 * HS, 4 * ROWS)
    return pl.pallas_call(
        attend_kernel,
        in_specs=[VMEM] * (10 + len(after)),
        out_shape=[shape(out, F32), shape(out), shape(out, F32), shape(out)],
        scratch_shapes=[pltpu.VMEM(wide, BF), pltpu.VMEM(wide, BF), pltpu.VMEM(wide, F32)],
        compiler_params=params(24),
        name="attend",
    )(*kv_blocks, *qd_blocks, mine, theirs, *after)


def gradient_kernel(qo_own, qo_got, kv_own, kv_got, *refs):
    own, pair, second, middle, ends = refs[:5]
    back, (keep, send, normed, d_proj, cut) = refs[5:9], refs[9:]
    at_end = (place[0] == 0) | (place[0] == 3)
    third = jnp.where(at_end, ends[...], middle[...])
    for k, block in enumerate((own[...], pair[...], second[...], third)):
        normed[k * ROWS : (k + 1) * ROWS, :] = normalise(block)[0].astype(BF)
    q_sum = qo_own[...] + qo_got[...].astype(F32)
    kv_sum = kv_own[...] + kv_got[...].astype(F32)
    d_proj[:HS, :] = q_sum[:HS].astype(BF)
    d_proj[HS : 3 * HS, :] = kv_sum.astype(BF)
    attended = q_sum[HS:].astype(BF)
    for k in range(4):
        at = slice(k * ROWS, (k + 1) * ROWS)
        back[k][: 3 * HS, :] = d_proj[:, at]
        back[k][3 * HS :, :] = attended[:, at]
    counts = [jnp.int32(0), jnp.int32(0)]
    for j in range(3):
        at = slice(j * HS, (j + 1) * HS)
        term = dot(d_proj[at, :], normed[...]).astype(BF)
        for i in range(4):
            unit = 16 * j + 4 * place[0] + i
            core = lax.rem(lax.div(unit, 3), 2)
            slot = jnp.where(core == 0, counts[0], counts[1])
            cut[core, slot] = term[i * 48 : (i + 1) * 48]
            counts = [counts[0] + (1 - core), counts[1] + core]
    keep[...] = cut[place[2]]
    send[...] = cut[1 - place[2]]


def gradient(qo_own, qo_got, kv_own, kv_got, tokens):
    units = (6, 48, D)
    return pl.pallas_call(
        gradient_kernel,
        in_specs=[VMEM] * 9,
        out_shape=[shape((4 * HS, ROWS))] * 4 + [shape(units)] * 2,
        scratch_shapes=[
            pltpu.VMEM((4 * ROWS, D), BF),
            pltpu.VMEM((3 * HS, 4 * ROWS), BF),
            pltpu.VMEM((2,) + units, BF),
        ],
        compiler_params=params(),
        name="gradient",
    )(qo_own, qo_got, kv_own, kv_got, *tokens)


WIDE = 512


def tokens_kernel(tokens, weights, *refs):
    blocks, (attended, d_tokens, done, columns, d_normed) = refs[:4], refs[4:]
    done[...] = jnp.zeros_like(done)
    for k in range(4):
        head = place[0] ^ k
        for j in range(4):
            at = pl.ds(pl.multiple_of(j * HD + head * HS, 64), HS)
            columns[at, :] = blocks[k][j * HS : (j + 1) * HS, :]
    attended[...] = flip(columns[3 * HD :, :]).astype(BF)
    d_proj = columns[: 3 * HD, :]
    unrounded, inverse = normalise(tokens[...])
    total = jnp.zeros((ROWS, 1), F32)
    for n in range(D // WIDE):
        at = slice(n * WIDE, (n + 1) * WIDE)
        part = jnp.transpose(dot(weights[at, :], d_proj))
        d_normed[:, at] = part
        total += jnp.sum(part * unrounded[:, at], -1, keepdims=True)
    d_tokens[...] = (inverse * (d_normed[...] - unrounded * (total * (1.0 / D)))).astype(BF)


def tokens_of(tokens, weights, blocks):
    return pl.pallas_call(
        tokens_kernel,
        in_specs=[VMEM] * 6,
        out_shape=[shape((ROWS, HD)), shape((ROWS, D)), shape((8, 128), F32)],
        scratch_shapes=[
            pltpu.VMEM((4 * HD, ROWS), BF),
            pltpu.VMEM((ROWS, D), F32),
        ],
        compiler_params=params(20),
        name="d_tokens",
    )(tokens, weights, *blocks)


def small(kernel, name, blocks, outs, scratch, after=()):
    return pl.pallas_call(
        kernel,
        in_specs=[VMEM] * (len(blocks) + len(after)),
        out_shape=outs,
        scratch_shapes=scratch,
        compiler_params=params(),
        name=name,
    )(*blocks, *after)


def split_y_kernel(mine, got, *refs):
    outs, cut = refs[:4], refs[4]
    cut[...] = (mine[...].astype(F32) + got[...].astype(F32)).astype(BF)
    for k in range(4):
        at = pl.ds(pl.multiple_of((place[1] ^ k) * 384, 384), 384)
        outs[k][...] = cut[:, :, at]


def ends_high(place):
    bits = jnp.int32(0)
    for head in range(HEADS):
        for core in range(2):
            units = [u for u in range(48) if u % 16 // 4 == head and u // 3 % 2 == core]
            value = sum((u // 6 % 2) << n for n, u in enumerate(units))
            bits = jnp.where((place[0] == head) & (place[2] == core), value, bits)
    return bits


def split_z_kernel(*refs):
    blocks, outs, cut = refs[:4], refs[4:8], refs[8]
    total = sum(block[...].astype(F32) for block in blocks)
    for k in range(4):
        cut[k] = total[:, :, k * 96 : (k + 1) * 96].astype(BF)
    bits = ends_high(place)
    for n in range(6):
        mirror = 3 * (((bits >> n) & 1) ^ place[4])
        for k in range(4):
            outs[k][n] = cut[place[0] ^ k ^ mirror, n]


def lists():
    tables = []
    for core in range(2):
        count, table = [0] * HEADS, []
        for slot in range(24):
            head = (6 * (slot // 3) + 3 * core + slot % 3) % 16 // 4
            table.append((head, count[head]))
            count[head] += 1
        tables.append(table)
    return list(zip(*tables))


def split_x_kernel(*refs):
    blocks, outs, by_head, cut = refs[:4], refs[4:8], refs[8], refs[9]
    for k in range(4):
        by_head[place[0] ^ k] = blocks[k][...]
    for slot, (first, second) in enumerate(lists()):
        head, at = (jnp.where(place[2] == 0, a, b) for a, b in zip(first, second))
        cut[slot] = by_head[head, at]
    for k in range(4):
        outs[k][...] = cut[pl.ds((place[3] ^ k) * 6, 6)]


def split_zh_kernel(*refs):
    blocks, (keep, send, cut) = refs[:4], refs[-3:]
    cut[...] = sum(block[...].astype(F32) for block in blocks)
    keep[...] = cut[pl.ds(place[4] * 3, 3)]
    send[...] = cut[pl.ds(3 - place[4] * 3, 3)].astype(BF)


def finish_kernel(mine, got, out):
    out[...] = (mine[...] + got[...].astype(F32)).reshape(144, 96)


def exchange(by):
    return [(i, i ^ by) for i in range(4)]


def per_device(tokens, w_proj, d_attended):
    tokens = tokens[0]
    near, far, swap = exchange(1), exchange(3), [(0, 1), (1, 0)]

    def spread(blocks, axis):
        return [blocks[0]] + [lax.ppermute(blocks[k], axis, exchange(k)) for k in (1, 2, 3)]

    pair = lax.ppermute(tokens, "zl", near)
    middle = lax.ppermute(tokens, "zl", [(1, 2), (2, 1)])
    heads = spread(project(tokens, w_proj, d_attended[0]), "zl")
    kv_a, qd_a = stack(heads[:2], [middle, pair])
    far_a, near_a = lax.ppermute(kv_a, "y", far), lax.ppermute(qd_a, "y", near)
    kv_b, qd_b = stack(heads[2:], [far_a, near_a])
    late = lax.optimization_barrier((tokens, kv_b))[0]
    second = lax.ppermute(late, "zl", exchange(2))
    ends = lax.ppermute(late, "zl", [(0, 3), (3, 0)])
    kv = [kv_a, kv_b, far_a, lax.ppermute(kv_b, "y", far)]
    qd = [qd_a, qd_b, near_a, lax.ppermute(qd_b, "y", near)]

    mine = stats_of(kv, qd)
    theirs = lax.ppermute(mine, "y", near)
    qo_own, qo_send, kv_own, kv_send = attend(kv, qd, mine, theirs, [ends])
    qo_got = lax.ppermute(qo_send, "y", near)
    kv_got = lax.ppermute(kv_send, "y", far)

    rows = [tokens, pair, second, middle, ends]
    *back, keep, send = gradient(qo_own, qo_got, kv_own, kv_got, rows)
    last = lax.ppermute(back[3], "zl", exchange(3))
    later = lax.optimization_barrier((back[2], last))[0]
    first, second = (lax.ppermute(b, "zl", exchange(k)) for k, b in ((1, back[1]), (2, later)))
    returned = [back[0], first, second, last]
    attended, d_tokens, done = tokens_of(tokens, w_proj, returned)
    got = lax.ppermute(send, "c", swap)
    blocks = small(
        split_y_kernel, "split_y", [keep, got],
        [shape((6, 48, 384))] * 4, [pltpu.VMEM((6, 48, D), BF)],
    )
    blocks = spread(blocks, "y")
    blocks = [blocks[k] for k in (0, 1, 3, 2)]
    blocks = small(
        split_z_kernel, "split_z", blocks,
        [shape((6, 48, 96))] * 4, [pltpu.VMEM((4, 6, 48, 96), BF)],
    )
    blocks = spread(blocks, "zl")
    blocks = small(
        split_x_kernel, "split_x", blocks,
        [shape((6, 48, 96))] * 4,
        [pltpu.VMEM((4, 6, 48, 96), BF), pltpu.VMEM((24, 48, 96), BF)],
    )
    blocks = spread(blocks, "x")
    blocks = [blocks[k] for k in (0, 1, 3, 2)]
    keep, send = small(
        split_zh_kernel, "split_zh", blocks,
        [shape((3, 48, 96), F32), shape((3, 48, 96))], [pltpu.VMEM((6, 48, 96), F32)], [done],
    )
    got = lax.ppermute(send, ("zh", "zl"), [(z, 7 - z) for z in range(8)])
    grad = small(finish_kernel, "finish", [keep, got], shape((144, 96), F32), [])
    return (attended[None], d_tokens[None], grad.T)


def solution(mesh):
    fine = Mesh(mesh.devices.reshape(4, 2, 2, 4, 4), ("x", "zh", "c", "y", "zl"))
    dp, seq = ("x", "zh", "c"), ("y", "zl")
    return jax.shard_map(
        per_device,
        mesh=fine,
        in_specs=(P(dp, seq, None), P(), P(dp, seq, None)),
        out_specs=(P(dp, seq, None), P(dp, seq, None), P(seq, dp)),
        check_vma=False,
    )
```

```python
import math

import jax
import jax.numpy as jnp
from jax import lax
from jax.experimental import pallas as pl
from jax.experimental.pallas import tpu as pltpu
from jax.sharding import Mesh
from jax.sharding import PartitionSpec as P

HS = 192
HEADS = 4
HD = 768
D = 1536
ROWS = 128
EPS = 1e-06
SCALE = 1.0 / math.sqrt(HS)
SCALE2 = SCALE * math.log2(math.e)
BF = jnp.bfloat16
F32 = jnp.float32
NN = (((1,), (0,)), ((), ()))
NT = (((1,), (1,)), ((), ()))

VMEM = pl.BlockSpec(memory_space=pltpu.VMEM)
ANY = pl.BlockSpec(memory_space=pl.ANY)
HBM = pl.BlockSpec(memory_space=pltpu.HBM)


def shape(dims, dtype=BF):
    return jax.ShapeDtypeStruct(dims, dtype)


class Place:
    def __getitem__(self, n):
        return lax.axis_index(("zl", "y", "c", "x", "zh")[n])


place = Place()


def params(mib=16):
    return pltpu.CompilerParams(vmem_limit_bytes=mib * 2**20)


def dot(a, b, dims=NN):
    return lax.dot_general(a, b, dims, preferred_element_type=F32)


def flip(block):
    return jnp.transpose(block.astype(F32))


def normalise(tokens):
    rows = tokens.astype(F32)
    inverse = lax.rsqrt(jnp.mean(rows * rows, -1, keepdims=True) + EPS)
    return rows * inverse, inverse


def project_kernel(tokens_in, weights_in, grads_in, *rest):
    blocks, (tokens, weights, grads, turned, sems) = rest[:4], rest[4:]
    fetches = [pltpu.make_async_copy(tokens_in, tokens, sems.at[0])]
    for j in range(3):
        at = slice(j * HD, (j + 1) * HD)
        fetches.append(pltpu.make_async_copy(weights_in.at[:, at], weights.at[j], sems.at[j + 1]))
    fetches.append(pltpu.make_async_copy(grads_in, grads, sems.at[4]))
    for fetch in fetches:
        fetch.start()
    fetches[0].wait()
    rows = normalise(tokens[...])[0].astype(BF)
    for j in range(3):
        fetches[j + 1].wait()
        turned[j * HD : (j + 1) * HD, :] = flip(dot(rows, weights[j])).astype(BF)
    fetches[4].wait()
    turned[3 * HD :, :] = flip(grads[...]).astype(BF)
    for k in range(4):
        head = place[0] ^ k
        for n, j in enumerate((1, 2, 0, 3)):
            at = pl.ds(pl.multiple_of(j * HD + head * HS, 64), HS)
            blocks[k][n * HS : (n + 1) * HS, :] = turned[at, :]


def project(tokens, weights, grads):
    return pl.pallas_call(
        project_kernel,
        in_specs=[HBM, HBM, HBM],
        out_specs=[VMEM] * 4,
        out_shape=[shape((4 * HS, ROWS))] * 4,
        scratch_shapes=[
            pltpu.VMEM((ROWS, D), BF),
            pltpu.VMEM((3, D, HD), BF),
            pltpu.VMEM((ROWS, HD), BF),
            pltpu.VMEM((4 * HD, ROWS), BF),
            pltpu.SemaphoreType.DMA((5,)),
        ],
        compiler_params=pltpu.CompilerParams(vmem_limit_bytes=62_520_000),
        name="project",
    )(tokens, weights, grads)


def stack_kernel(*refs):
    kv, qd = refs[-2:]
    for k, block in enumerate(refs[:2]):
        at = slice(k * ROWS, (k + 1) * ROWS)
        kv[:, at] = block[: 2 * HS, :]
        qd[:, at] = block[2 * HS :, :]


def stack(blocks, after=()):
    return pl.pallas_call(
        stack_kernel,
        in_specs=[VMEM] * 2 + [ANY] * len(after),
        out_shape=[shape((2 * HS, 2 * ROWS))] * 2,
        compiler_params=params(),
        name="stack",
    )(*blocks, *after)


def side_by_side(blocks, wide):
    for k, block in enumerate(blocks):
        wide[:, k * 2 * ROWS : (k + 1) * 2 * ROWS] = block[...]


TILE = 256


def stats_kernel(*refs):
    kv_blocks, qd_blocks, (stats, kv, qd) = refs[:4], refs[4:8], refs[-3:]
    side_by_side(kv_blocks, kv)
    side_by_side(qd_blocks, qd)
    keys = flip(kv[:HS, :]).astype(BF)
    values = flip(kv[HS:, :]).astype(BF)
    for tile in range(8 * ROWS // TILE):
        at = slice(tile * TILE, (tile + 1) * TILE)
        scores = dot(keys, qd[:HS, at]) * SCALE2
        top = jnp.max(scores, 0, keepdims=True)
        powers = jnp.exp2(scores - top)
        d_probs = dot(values, qd[HS:, at])
        stats[0:1, at] = top
        stats[1:2, at] = jnp.sum(powers, 0, keepdims=True)
        stats[2:3, at] = jnp.sum(powers * d_probs, 0, keepdims=True)
        stats[3:8, at] = jnp.zeros((5, TILE), F32)


def stats_of(kv_blocks, qd_blocks):
    wide = pltpu.VMEM((2 * HS, 8 * ROWS), BF)
    return pl.pallas_call(
        stats_kernel,
        out_shape=shape((8, 8 * ROWS), F32),
        scratch_shapes=[wide, wide],
        compiler_params=params(),
        name="stats",
    )(*kv_blocks, *qd_blocks)


def attend_kernel(*refs):
    kv_blocks, qd_blocks, mine, theirs = refs[:4], refs[4:8], refs[8], refs[9]
    qo_own, qo_send, kv_own, kv_send, kv, qd, kv_sum = refs[-7:]
    side_by_side(kv_blocks, kv)
    side_by_side(qd_blocks, qd)
    keys = flip(kv[:HS, :]).astype(BF)
    values = flip(kv[HS:, :]).astype(BF)
    half = 4 * ROWS
    for tile in range(8 * ROWS // TILE):
        at = slice(tile * TILE, (tile + 1) * TILE)
        start = (tile * TILE + half) % (2 * half)
        across = slice(start, start + TILE)
        top_a, sum_a, total_a = mine[0:1, at], mine[1:2, at], mine[2:3, at]
        top_b, sum_b, total_b = theirs[0:1, across], theirs[1:2, across], theirs[2:3, across]
        top = jnp.maximum(top_a, top_b)
        by_a, by_b = jnp.exp2(top_a - top), jnp.exp2(top_b - top)
        share = 1.0 / (sum_a * by_a + sum_b * by_b)
        row_total = (total_a * by_a + total_b * by_b) * share
        scores = dot(keys, qd[:HS, at]) * SCALE2
        softmaxed = jnp.exp2(scores - top) * share
        d_probs = dot(values, qd[HS:, at])
        d_scores = (softmaxed * (d_probs - row_total) * SCALE).astype(BF)
        weights = softmaxed.astype(BF)
        d_queries = dot(kv[:HS, :], d_scores)
        attended = dot(kv[HS:, :], weights)
        if tile * TILE < half:
            qo_own[:HS, at] = d_queries
            qo_own[HS:, at] = attended
        else:
            qo_send[:HS, across] = d_queries.astype(BF)
            qo_send[HS:, across] = attended.astype(BF)
        d_keys = dot(qd[:HS, at], d_scores, NT)
        d_values = dot(qd[HS:, at], weights, NT)
        if tile == 0:
            kv_sum[:HS, :] = d_keys
            kv_sum[HS:, :] = d_values
        else:
            kv_sum[:HS, :] += d_keys
            kv_sum[HS:, :] += d_values
    kv_own[...] = kv_sum[:, :half]
    kv_send[...] = kv_sum[:, half:].astype(BF)


def attend(kv_blocks, qd_blocks, mine, theirs, after):
    wide = (2 * HS, 8 * ROWS)
    out = (2 * HS, 4 * ROWS)
    return pl.pallas_call(
        attend_kernel,
        in_specs=[VMEM] * (10 + len(after)),
        out_shape=[shape(out, F32), shape(out), shape(out, F32), shape(out)],
        scratch_shapes=[pltpu.VMEM(wide, BF), pltpu.VMEM(wide, BF), pltpu.VMEM(wide, F32)],
        compiler_params=params(24),
        name="attend",
    )(*kv_blocks, *qd_blocks, mine, theirs, *after)


def gradient_kernel(qo_own, qo_got, kv_own, kv_got, *refs):
    own, pair, second, middle, ends = refs[:5]
    back, (keep, send, normed, d_proj, cut) = refs[5:9], refs[9:]
    at_end = (place[0] == 0) | (place[0] == 3)
    third = jnp.where(at_end, ends[...], middle[...])
    for k, block in enumerate((own[...], pair[...], second[...], third)):
        normed[k * ROWS : (k + 1) * ROWS, :] = normalise(block)[0].astype(BF)
    q_sum = qo_own[...] + qo_got[...].astype(F32)
    kv_sum = kv_own[...] + kv_got[...].astype(F32)
    d_proj[:HS, :] = q_sum[:HS].astype(BF)
    d_proj[HS : 3 * HS, :] = kv_sum.astype(BF)
    attended = q_sum[HS:].astype(BF)
    for k in range(4):
        at = slice(k * ROWS, (k + 1) * ROWS)
        back[k][: 3 * HS, :] = d_proj[:, at]
        back[k][3 * HS :, :] = attended[:, at]
    counts = [jnp.int32(0), jnp.int32(0)]
    for j in range(3):
        at = slice(j * HS, (j + 1) * HS)
        term = dot(d_proj[at, :], normed[...]).astype(BF)
        for i in range(4):
            unit = 16 * j + 4 * place[0] + i
            core = lax.rem(lax.div(unit, 3), 2)
            slot = jnp.where(core == 0, counts[0], counts[1])
            cut[core, slot] = term[i * 48 : (i + 1) * 48]
            counts = [counts[0] + (1 - core), counts[1] + core]
    keep[...] = cut[place[2]]
    send[...] = cut[1 - place[2]]


def gradient(qo_own, qo_got, kv_own, kv_got, tokens):
    units = (6, 48, D)
    return pl.pallas_call(
        gradient_kernel,
        in_specs=[VMEM] * 9,
        out_shape=[shape((4 * HS, ROWS))] * 4 + [shape(units)] * 2,
        scratch_shapes=[
            pltpu.VMEM((4 * ROWS, D), BF),
            pltpu.VMEM((3 * HS, 4 * ROWS), BF),
            pltpu.VMEM((2,) + units, BF),
        ],
        compiler_params=params(),
        name="gradient",
    )(qo_own, qo_got, kv_own, kv_got, *tokens)


WIDE = 512


def tokens_kernel(tokens, weights, *refs):
    blocks, (attended, d_tokens, done, columns, d_normed) = refs[:4], refs[4:]
    done[...] = jnp.zeros_like(done)
    for k in range(4):
        head = place[0] ^ k
        for j in range(4):
            at = pl.ds(pl.multiple_of(j * HD + head * HS, 64), HS)
            columns[at, :] = blocks[k][j * HS : (j + 1) * HS, :]
    attended[...] = flip(columns[3 * HD :, :]).astype(BF)
    d_proj = columns[: 3 * HD, :]
    unrounded, inverse = normalise(tokens[...])
    total = jnp.zeros((ROWS, 1), F32)
    for n in range(D // WIDE):
        at = slice(n * WIDE, (n + 1) * WIDE)
        part = jnp.transpose(dot(weights[at, :], d_proj))
        d_normed[:, at] = part
        total += jnp.sum(part * unrounded[:, at], -1, keepdims=True)
    d_tokens[...] = (inverse * (d_normed[...] - unrounded * (total * (1.0 / D)))).astype(BF)


def tokens_of(tokens, weights, blocks):
    return pl.pallas_call(
        tokens_kernel,
        in_specs=[VMEM] * 6,
        out_shape=[shape((ROWS, HD)), shape((ROWS, D)), shape((8, 128), F32)],
        scratch_shapes=[
            pltpu.VMEM((4 * HD, ROWS), BF),
            pltpu.VMEM((ROWS, D), F32),
        ],
        compiler_params=params(20),
        name="d_tokens",
    )(tokens, weights, *blocks)


def small(kernel, name, blocks, outs, scratch, after=()):
    return pl.pallas_call(
        kernel,
        in_specs=[VMEM] * (len(blocks) + len(after)),
        out_shape=outs,
        scratch_shapes=scratch,
        compiler_params=params(),
        name=name,
    )(*blocks, *after)


def split_y_kernel(mine, got, *refs):
    outs, cut = refs[:4], refs[4]
    cut[...] = (mine[...].astype(F32) + got[...].astype(F32)).astype(BF)
    for k in range(4):
        at = pl.ds(pl.multiple_of((place[1] ^ k) * 384, 384), 384)
        outs[k][...] = cut[:, :, at]


def ends_high(place):
    bits = jnp.int32(0)
    for head in range(HEADS):
        for core in range(2):
            units = [u for u in range(48) if u % 16 // 4 == head and u // 3 % 2 == core]
            value = sum((u // 6 % 2) << n for n, u in enumerate(units))
            bits = jnp.where((place[0] == head) & (place[2] == core), value, bits)
    return bits


def split_z_kernel(*refs):
    blocks, outs, cut = refs[:4], refs[4:8], refs[8]
    total = sum(block[...].astype(F32) for block in blocks)
    for k in range(4):
        cut[k] = total[:, :, k * 96 : (k + 1) * 96].astype(BF)
    bits = ends_high(place)
    for n in range(6):
        mirror = 3 * (((bits >> n) & 1) ^ place[4])
        for k in range(4):
            outs[k][n] = cut[place[0] ^ k ^ mirror, n]


def lists():
    tables = []
    for core in range(2):
        count, table = [0] * HEADS, []
        for slot in range(24):
            head = (6 * (slot // 3) + 3 * core + slot % 3) % 16 // 4
            table.append((head, count[head]))
            count[head] += 1
        tables.append(table)
    return list(zip(*tables))


def split_x_kernel(*refs):
    blocks, outs, by_head, cut = refs[:4], refs[4:8], refs[8], refs[9]
    for k in range(4):
        by_head[place[0] ^ k] = blocks[k][...]
    for slot, (first, second) in enumerate(lists()):
        head, at = (jnp.where(place[2] == 0, a, b) for a, b in zip(first, second))
        cut[slot] = by_head[head, at]
    for k in range(4):
        outs[k][...] = cut[pl.ds((place[3] ^ k) * 6, 6)]


def split_zh_kernel(*refs):
    blocks, (keep, send, cut) = refs[:4], refs[-3:]
    cut[...] = sum(block[...].astype(F32) for block in blocks)
    keep[...] = cut[pl.ds(place[4] * 3, 3)]
    send[...] = cut[pl.ds(3 - place[4] * 3, 3)].astype(BF)


def finish_kernel(mine, got, out):
    out[...] = (mine[...] + got[...].astype(F32)).reshape(144, 96)


def exchange(by):
    return [(i, i ^ by) for i in range(4)]


def per_device(tokens, w_proj, d_attended):
    tokens = tokens[0]
    near, far, swap = exchange(1), exchange(3), [(0, 1), (1, 0)]

    def spread(blocks, axis):
        return [blocks[0]] + [lax.ppermute(blocks[k], axis, exchange(k)) for k in (1, 2, 3)]

    middle = lax.ppermute(tokens, "zl", [(1, 2), (2, 1)])
    heads = spread(project(tokens, w_proj, d_attended[0]), "zl")
    kv_a, qd_a = stack(heads[:2], [middle])
    far_a, near_a = lax.ppermute(kv_a, "y", far), lax.ppermute(qd_a, "y", near)
    kv_b, qd_b = stack(heads[2:], [far_a, near_a])
    late = lax.optimization_barrier((tokens, kv_b))[0]
    pair = lax.ppermute(late, "zl", near)
    second = lax.ppermute(late, "zl", exchange(2))
    ends = lax.ppermute(late, "zl", [(0, 3), (3, 0)])
    kv = [kv_a, kv_b, far_a, lax.ppermute(kv_b, "y", far)]
    qd = [qd_a, qd_b, near_a, lax.ppermute(qd_b, "y", near)]

    mine = stats_of(kv, qd)
    theirs = lax.ppermute(mine, "y", near)
    qo_own, qo_send, kv_own, kv_send = attend(kv, qd, mine, theirs, [ends])
    qo_got = lax.ppermute(qo_send, "y", near)
    kv_got = lax.ppermute(kv_send, "y", far)

    rows = [tokens, pair, second, middle, ends]
    *back, keep, send = gradient(qo_own, qo_got, kv_own, kv_got, rows)
    last = lax.ppermute(back[3], "zl", exchange(3))
    later = lax.optimization_barrier((back[2], last))[0]
    first, second = (lax.ppermute(b, "zl", exchange(k)) for k, b in ((1, back[1]), (2, later)))
    returned = [back[0], first, second, last]
    attended, d_tokens, done = tokens_of(tokens, w_proj, returned)
    got = lax.ppermute(send, "c", swap)
    blocks = small(
        split_y_kernel, "split_y", [keep, got],
        [shape((6, 48, 384))] * 4, [pltpu.VMEM((6, 48, D), BF)],
    )
    blocks = spread(blocks, "y")
    blocks = [blocks[k] for k in (0, 1, 3, 2)]
    blocks = small(
        split_z_kernel, "split_z", blocks,
        [shape((6, 48, 96))] * 4, [pltpu.VMEM((4, 6, 48, 96), BF)],
    )
    blocks = spread(blocks, "zl")
    blocks = small(
        split_x_kernel, "split_x", blocks,
        [shape((6, 48, 96))] * 4,
        [pltpu.VMEM((4, 6, 48, 96), BF), pltpu.VMEM((24, 48, 96), BF)],
    )
    blocks = spread(blocks, "x")
    blocks = [blocks[k] for k in (0, 1, 3, 2)]
    keep, send = small(
        split_zh_kernel, "split_zh", blocks,
        [shape((3, 48, 96), F32), shape((3, 48, 96))], [pltpu.VMEM((6, 48, 96), F32)], [done],
    )
    got = lax.ppermute(send, ("zh", "zl"), [(z, 7 - z) for z in range(8)])
    grad = small(finish_kernel, "finish", [keep, got], shape((144, 96), F32), [])
    return (attended[None], d_tokens[None], grad.T)


def solution(mesh):
    fine = Mesh(mesh.devices.reshape(4, 2, 2, 4, 4), ("x", "zh", "c", "y", "zl"))
    dp, seq = ("x", "zh", "c"), ("y", "zl")
    return jax.shard_map(
        per_device,
        mesh=fine,
        in_specs=(P(dp, seq, None), P(), P(dp, seq, None)),
        out_specs=(P(dp, seq, None), P(dp, seq, None), P(seq, dp)),
        check_vma=False,
    )
```

```python
import math

import jax
import jax.numpy as jnp
from jax import lax
from jax.experimental import pallas as pl
from jax.experimental.pallas import tpu as pltpu
from jax.sharding import Mesh
from jax.sharding import PartitionSpec as P

HS = 192
HEADS = 4
HD = 768
D = 1536
ROWS = 128
EPS = 1e-06
SCALE = 1.0 / math.sqrt(HS)
SCALE2 = SCALE * math.log2(math.e)
BF = jnp.bfloat16
F32 = jnp.float32
NN = (((1,), (0,)), ((), ()))
NT = (((1,), (1,)), ((), ()))

VMEM = pl.BlockSpec(memory_space=pltpu.VMEM)
ANY = pl.BlockSpec(memory_space=pl.ANY)
HBM = pl.BlockSpec(memory_space=pltpu.HBM)


def shape(dims, dtype=BF):
    return jax.ShapeDtypeStruct(dims, dtype)


class Place:
    def __getitem__(self, n):
        return lax.axis_index(("zl", "y", "c", "x", "zh")[n])


place = Place()


def params(mib=16):
    return pltpu.CompilerParams(vmem_limit_bytes=mib * 2**20)


def dot(a, b, dims=NN):
    return lax.dot_general(a, b, dims, preferred_element_type=F32)


def flip(block):
    return jnp.transpose(block.astype(F32))


def normalise(tokens):
    rows = tokens.astype(F32)
    inverse = lax.rsqrt(jnp.mean(rows * rows, -1, keepdims=True) + EPS)
    return rows * inverse, inverse


def project_kernel(tokens_in, weights_in, grads_in, *rest):
    blocks, (tokens, weights, grads, turned, sems) = rest[:4], rest[4:]
    fetches = [pltpu.make_async_copy(tokens_in, tokens, sems.at[0])]
    for j in range(3):
        at = slice(j * HD, (j + 1) * HD)
        fetches.append(pltpu.make_async_copy(weights_in.at[:, at], weights.at[j], sems.at[j + 1]))
    fetches.append(pltpu.make_async_copy(grads_in, grads, sems.at[4]))
    for fetch in fetches:
        fetch.start()
    fetches[0].wait()
    rows = normalise(tokens[...])[0].astype(BF)
    for j in range(3):
        fetches[j + 1].wait()
        turned[j * HD : (j + 1) * HD, :] = flip(dot(rows, weights[j])).astype(BF)
    fetches[4].wait()
    turned[3 * HD :, :] = flip(grads[...]).astype(BF)
    for k in range(4):
        head = place[0] ^ k
        for n, j in enumerate((1, 2, 0, 3)):
            at = pl.ds(pl.multiple_of(j * HD + head * HS, 64), HS)
            blocks[k][n * HS : (n + 1) * HS, :] = turned[at, :]


def project(tokens, weights, grads):
    return pl.pallas_call(
        project_kernel,
        in_specs=[HBM, HBM, HBM],
        out_specs=[VMEM] * 4,
        out_shape=[shape((4 * HS, ROWS))] * 4,
        scratch_shapes=[
            pltpu.VMEM((ROWS, D), BF),
            pltpu.VMEM((3, D, HD), BF),
            pltpu.VMEM((ROWS, HD), BF),
            pltpu.VMEM((4 * HD, ROWS), BF),
            pltpu.SemaphoreType.DMA((5,)),
        ],
        compiler_params=pltpu.CompilerParams(vmem_limit_bytes=62_520_000),
        name="project",
    )(tokens, weights, grads)


def stack_kernel(*refs):
    kv, qd = refs[-2:]
    for k, block in enumerate(refs[:2]):
        at = slice(k * ROWS, (k + 1) * ROWS)
        kv[:, at] = block[: 2 * HS, :]
        qd[:, at] = block[2 * HS :, :]


def stack(blocks, after=()):
    return pl.pallas_call(
        stack_kernel,
        in_specs=[VMEM] * 2 + [ANY] * len(after),
        out_shape=[shape((2 * HS, 2 * ROWS))] * 2,
        compiler_params=params(),
        name="stack",
    )(*blocks, *after)


def side_by_side(blocks, wide):
    for k, block in enumerate(blocks):
        wide[:, k * 2 * ROWS : (k + 1) * 2 * ROWS] = block[...]


TILE = 256


def stats_kernel(*refs):
    kv_blocks, qd_blocks, (stats, kv, qd) = refs[:4], refs[4:8], refs[-3:]
    side_by_side(kv_blocks, kv)
    side_by_side(qd_blocks, qd)
    keys = flip(kv[:HS, :]).astype(BF)
    values = flip(kv[HS:, :]).astype(BF)
    for tile in range(8 * ROWS // TILE):
        at = slice(tile * TILE, (tile + 1) * TILE)
        scores = dot(keys, qd[:HS, at]) * SCALE2
        top = jnp.max(scores, 0, keepdims=True)
        powers = jnp.exp2(scores - top)
        d_probs = dot(values, qd[HS:, at])
        stats[0:1, at] = top
        stats[1:2, at] = jnp.sum(powers, 0, keepdims=True)
        stats[2:3, at] = jnp.sum(powers * d_probs, 0, keepdims=True)
        stats[3:8, at] = jnp.zeros((5, TILE), F32)


def stats_of(kv_blocks, qd_blocks):
    wide = pltpu.VMEM((2 * HS, 8 * ROWS), BF)
    return pl.pallas_call(
        stats_kernel,
        out_shape=shape((8, 8 * ROWS), F32),
        scratch_shapes=[wide, wide],
        compiler_params=params(),
        name="stats",
    )(*kv_blocks, *qd_blocks)


def attend_kernel(*refs):
    kv_blocks, qd_blocks, mine, theirs = refs[:4], refs[4:8], refs[8], refs[9]
    qo_own, qo_send, kv_own, kv_send, kv, qd, kv_sum = refs[-7:]
    side_by_side(kv_blocks, kv)
    side_by_side(qd_blocks, qd)
    keys = flip(kv[:HS, :]).astype(BF)
    values = flip(kv[HS:, :]).astype(BF)
    half = 4 * ROWS
    for tile in range(8 * ROWS // TILE):
        at = slice(tile * TILE, (tile + 1) * TILE)
        start = (tile * TILE + half) % (2 * half)
        across = slice(start, start + TILE)
        top_a, sum_a, total_a = mine[0:1, at], mine[1:2, at], mine[2:3, at]
        top_b, sum_b, total_b = theirs[0:1, across], theirs[1:2, across], theirs[2:3, across]
        top = jnp.maximum(top_a, top_b)
        by_a, by_b = jnp.exp2(top_a - top), jnp.exp2(top_b - top)
        share = 1.0 / (sum_a * by_a + sum_b * by_b)
        row_total = (total_a * by_a + total_b * by_b) * share
        scores = dot(keys, qd[:HS, at]) * SCALE2
        softmaxed = jnp.exp2(scores - top) * share
        d_probs = dot(values, qd[HS:, at])
        d_scores = (softmaxed * (d_probs - row_total) * SCALE).astype(BF)
        weights = softmaxed.astype(BF)
        d_queries = dot(kv[:HS, :], d_scores)
        attended = dot(kv[HS:, :], weights)
        if tile * TILE < half:
            qo_own[:HS, at] = d_queries
            qo_own[HS:, at] = attended
        else:
            qo_send[:HS, across] = d_queries.astype(BF)
            qo_send[HS:, across] = attended.astype(BF)
        d_keys = dot(qd[:HS, at], d_scores, NT)
        d_values = dot(qd[HS:, at], weights, NT)
        if tile == 0:
            kv_sum[:HS, :] = d_keys
            kv_sum[HS:, :] = d_values
        else:
            kv_sum[:HS, :] += d_keys
            kv_sum[HS:, :] += d_values
    kv_own[...] = kv_sum[:, :half]
    kv_send[...] = kv_sum[:, half:].astype(BF)


def attend(kv_blocks, qd_blocks, mine, theirs, after):
    wide = (2 * HS, 8 * ROWS)
    out = (2 * HS, 4 * ROWS)
    return pl.pallas_call(
        attend_kernel,
        in_specs=[VMEM] * (10 + len(after)),
        out_shape=[shape(out, F32), shape(out), shape(out, F32), shape(out)],
        scratch_shapes=[pltpu.VMEM(wide, BF), pltpu.VMEM(wide, BF), pltpu.VMEM(wide, F32)],
        compiler_params=params(24),
        name="attend",
    )(*kv_blocks, *qd_blocks, mine, theirs, *after)


def gradient_kernel(qo_own, qo_got, kv_own, kv_got, *refs):
    own, pair, second, middle, ends = refs[:5]
    back, (keep, send, normed, d_proj, cut) = refs[5:9], refs[9:]
    at_end = (place[0] == 0) | (place[0] == 3)
    third = jnp.where(at_end, ends[...], middle[...])
    for k, block in enumerate((own[...], pair[...], second[...], third)):
        normed[k * ROWS : (k + 1) * ROWS, :] = normalise(block)[0].astype(BF)
    q_sum = qo_own[...] + qo_got[...].astype(F32)
    kv_sum = kv_own[...] + kv_got[...].astype(F32)
    d_proj[:HS, :] = q_sum[:HS].astype(BF)
    d_proj[HS : 3 * HS, :] = kv_sum.astype(BF)
    attended = q_sum[HS:].astype(BF)
    for k in range(4):
        at = slice(k * ROWS, (k + 1) * ROWS)
        back[k][: 3 * HS, :] = d_proj[:, at]
        back[k][3 * HS :, :] = attended[:, at]
    counts = [jnp.int32(0), jnp.int32(0)]
    for j in range(3):
        at = slice(j * HS, (j + 1) * HS)
        term = dot(d_proj[at, :], normed[...]).astype(BF)
        for i in range(4):
            unit = 16 * j + 4 * place[0] + i
            core = lax.rem(lax.div(unit, 3), 2)
            slot = jnp.where(core == 0, counts[0], counts[1])
            cut[core, slot] = term[i * 48 : (i + 1) * 48]
            counts = [counts[0] + (1 - core), counts[1] + core]
    keep[...] = cut[place[2]]
    send[...] = cut[1 - place[2]]


def gradient(qo_own, qo_got, kv_own, kv_got, tokens):
    units = (6, 48, D)
    return pl.pallas_call(
        gradient_kernel,
        in_specs=[VMEM] * 9,
        out_shape=[shape((4 * HS, ROWS))] * 4 + [shape(units)] * 2,
        scratch_shapes=[
            pltpu.VMEM((4 * ROWS, D), BF),
            pltpu.VMEM((3 * HS, 4 * ROWS), BF),
            pltpu.VMEM((2,) + units, BF),
        ],
        compiler_params=params(),
        name="gradient",
    )(qo_own, qo_got, kv_own, kv_got, *tokens)


WIDE = 512


def tokens_kernel(tokens, weights, *refs):
    blocks, (attended, d_tokens, done, columns, d_normed) = refs[:4], refs[4:]
    done[...] = jnp.zeros_like(done)
    for k in range(4):
        head = place[0] ^ k
        for j in range(4):
            at = pl.ds(pl.multiple_of(j * HD + head * HS, 64), HS)
            columns[at, :] = blocks[k][j * HS : (j + 1) * HS, :]
    attended[...] = flip(columns[3 * HD :, :]).astype(BF)
    d_proj = columns[: 3 * HD, :]
    unrounded, inverse = normalise(tokens[...])
    total = jnp.zeros((ROWS, 1), F32)
    for n in range(D // WIDE):
        at = slice(n * WIDE, (n + 1) * WIDE)
        part = jnp.transpose(dot(weights[at, :], d_proj))
        d_normed[:, at] = part
        total += jnp.sum(part * unrounded[:, at], -1, keepdims=True)
    d_tokens[...] = (inverse * (d_normed[...] - unrounded * (total * (1.0 / D)))).astype(BF)


def tokens_of(tokens, weights, blocks):
    return pl.pallas_call(
        tokens_kernel,
        in_specs=[VMEM] * 6,
        out_shape=[shape((ROWS, HD)), shape((ROWS, D)), shape((8, 128), F32)],
        scratch_shapes=[
            pltpu.VMEM((4 * HD, ROWS), BF),
            pltpu.VMEM((ROWS, D), F32),
        ],
        compiler_params=params(20),
        name="d_tokens",
    )(tokens, weights, *blocks)


def small(kernel, name, blocks, outs, scratch, after=()):
    return pl.pallas_call(
        kernel,
        in_specs=[VMEM] * (len(blocks) + len(after)),
        out_shape=outs,
        scratch_shapes=scratch,
        compiler_params=params(),
        name=name,
    )(*blocks, *after)


def split_y_kernel(mine, got, *refs):
    outs, cut = refs[:4], refs[4]
    cut[...] = (mine[...].astype(F32) + got[...].astype(F32)).astype(BF)
    for k in range(4):
        at = pl.ds(pl.multiple_of((place[1] ^ k) * 384, 384), 384)
        outs[k][...] = cut[:, :, at]


def ends_high(place):
    bits = jnp.int32(0)
    for head in range(HEADS):
        for core in range(2):
            units = [u for u in range(48) if u % 16 // 4 == head and u // 3 % 2 == core]
            value = sum((u // 6 % 2) << n for n, u in enumerate(units))
            bits = jnp.where((place[0] == head) & (place[2] == core), value, bits)
    return bits


def split_z_kernel(*refs):
    blocks, outs, cut = refs[:4], refs[4:8], refs[8]
    total = sum(block[...].astype(F32) for block in blocks)
    for k in range(4):
        cut[k] = total[:, :, k * 96 : (k + 1) * 96].astype(BF)
    bits = ends_high(place)
    for n in range(6):
        mirror = 3 * (((bits >> n) & 1) ^ place[4])
        for k in range(4):
            outs[k][n] = cut[place[0] ^ k ^ mirror, n]


def lists():
    tables = []
    for core in range(2):
        count, table = [0] * HEADS, []
        for slot in range(24):
            head = (6 * (slot // 3) + 3 * core + slot % 3) % 16 // 4
            table.append((head, count[head]))
            count[head] += 1
        tables.append(table)
    return list(zip(*tables))


FAR_FIRST = (0, 3, 2, 1)


def split_x_kernel(*refs):
    blocks, outs, by_head, cut = refs[:4], refs[4:8], refs[8], refs[9]
    for k in range(4):
        by_head[place[0] ^ FAR_FIRST[k]] = blocks[k][...]
    for slot, (first, second) in enumerate(lists()):
        head, at = (jnp.where(place[2] == 0, a, b) for a, b in zip(first, second))
        cut[slot] = by_head[head, at]
    for k in range(4):
        outs[k][...] = cut[pl.ds((place[3] ^ k) * 6, 6)]


def split_zh_kernel(*refs):
    blocks, (keep, send, cut) = refs[:4], refs[-3:]
    cut[...] = sum(block[...].astype(F32) for block in blocks)
    keep[...] = cut[pl.ds(place[4] * 3, 3)]
    send[...] = cut[pl.ds(3 - place[4] * 3, 3)].astype(BF)


def finish_kernel(mine, got, out):
    out[...] = (mine[...] + got[...].astype(F32)).reshape(144, 96)


def exchange(by):
    return [(i, i ^ by) for i in range(4)]


def per_device(tokens, w_proj, d_attended):
    tokens = tokens[0]
    near, far, swap = exchange(1), exchange(3), [(0, 1), (1, 0)]

    def spread(blocks, axis):
        return [blocks[0]] + [lax.ppermute(blocks[k], axis, exchange(k)) for k in (1, 2, 3)]

    middle = lax.ppermute(tokens, "zl", [(1, 2), (2, 1)])
    heads = spread(project(tokens, w_proj, d_attended[0]), "zl")
    kv_a, qd_a = stack(heads[:2], [middle])
    far_a, near_a = lax.ppermute(kv_a, "y", far), lax.ppermute(qd_a, "y", near)
    kv_b, qd_b = stack(heads[2:], [far_a, near_a])
    late = lax.optimization_barrier((tokens, kv_b))[0]
    pair = lax.ppermute(late, "zl", near)
    second = lax.ppermute(late, "zl", exchange(2))
    ends = lax.ppermute(late, "zl", [(0, 3), (3, 0)])
    kv = [kv_a, kv_b, far_a, lax.ppermute(kv_b, "y", far)]
    qd = [qd_a, qd_b, near_a, lax.ppermute(qd_b, "y", near)]

    mine = stats_of(kv, qd)
    theirs = lax.ppermute(mine, "y", near)
    qo_own, qo_send, kv_own, kv_send = attend(kv, qd, mine, theirs, [ends])
    qo_got = lax.ppermute(qo_send, "y", near)
    kv_got = lax.ppermute(kv_send, "y", far)

    rows = [tokens, pair, second, middle, ends]
    *back, keep, send = gradient(qo_own, qo_got, kv_own, kv_got, rows)
    last = lax.ppermute(back[3], "zl", exchange(3))
    later = lax.optimization_barrier((back[2], last))[0]
    first, second = (lax.ppermute(b, "zl", exchange(k)) for k, b in ((1, back[1]), (2, later)))
    returned = [back[0], first, second, last]
    attended, d_tokens, done = tokens_of(tokens, w_proj, returned)
    got = lax.ppermute(send, "c", swap)
    blocks = small(
        split_y_kernel, "split_y", [keep, got],
        [shape((6, 48, 384))] * 4, [pltpu.VMEM((6, 48, D), BF)],
    )
    blocks = spread(blocks, "y")
    blocks = [blocks[k] for k in (0, 2, 1, 3)]
    blocks = small(
        split_z_kernel, "split_z", blocks,
        [shape((6, 48, 96))] * 4, [pltpu.VMEM((4, 6, 48, 96), BF)],
    )
    blocks = spread(blocks, "zl")
    blocks = [blocks[k] for k in FAR_FIRST]
    blocks = small(
        split_x_kernel, "split_x", blocks,
        [shape((6, 48, 96))] * 4,
        [pltpu.VMEM((4, 6, 48, 96), BF), pltpu.VMEM((24, 48, 96), BF)],
    )
    blocks = spread(blocks, "x")
    blocks = [blocks[k] for k in (0, 2, 1, 3)]
    keep, send = small(
        split_zh_kernel, "split_zh", blocks,
        [shape((3, 48, 96), F32), shape((3, 48, 96))], [pltpu.VMEM((6, 48, 96), F32)], [done],
    )
    got = lax.ppermute(send, ("zh", "zl"), [(z, 7 - z) for z in range(8)])
    grad = small(finish_kernel, "finish", [keep, got], shape((144, 96), F32), [])
    return (attended[None], d_tokens[None], grad.T)


def solution(mesh):
    fine = Mesh(mesh.devices.reshape(4, 2, 2, 4, 4), ("x", "zh", "c", "y", "zl"))
    dp, seq = ("x", "zh", "c"), ("y", "zl")
    return jax.shard_map(
        per_device,
        mesh=fine,
        in_specs=(P(dp, seq, None), P(), P(dp, seq, None)),
        out_specs=(P(dp, seq, None), P(dp, seq, None), P(seq, dp)),
        check_vma=False,
    )
```
